256 devices in a mesh: dp: 8 (over x, z_lo), ctx: 32 (over y, z_hi, core).
Axes of the slice: x: 4, y: 4, z: 8 (z_hi: 4, z_lo: 2; z = z_hi * 2 + z_lo), core: 2. Of those that a mesh axis runs over, the one named last changes fastest.
Arguments:
- cont_query: bfloat16 [81920, 1536], P(('dp', 'ctx')), parts along dimension 0, may hold values from -8 to 8
- cont_key: bfloat16 [81920, 1536], P(('dp', 'ctx')), parts along dimension 0, may hold values from -6 to 6
- cont_value: bfloat16 [81920, 1536], P(('dp', 'ctx')), parts along dimension 0, may hold values from -6 to 6
- prompt_key: bfloat16 [65536, 1536], P(('dp', 'ctx')), parts along dimension 0, may hold values from -8 to 8
- prompt_value: bfloat16 [65536, 1536], P(('dp', 'ctx')), parts along dimension 0, may hold values from -6 to 6
- out_grad: bfloat16 [81920, 1536], P(('dp', 'ctx')), parts along dimension 0, may hold values from -6 to 6
- prompt_links: int32 [256, 3], P(('dp', 'ctx')), parts along dimension 0, may hold values from 0 to 1, as said below
- cont_start: int32 [256], P(('dp', 'ctx')), parts along dimension 0, may hold values from 0 to 31, as said below
- valid_len: int32 [256], P('dp'), parts along dimension 0, may hold values from 80 to 320, as said below
Outputs:
- attended: bfloat16 [81920, 1536], P(('dp', 'ctx')), parts along dimension 0
- query_grad: bfloat16 [81920, 1536], P(('dp', 'ctx')), parts along dimension 0
- cont_key_grad: bfloat16 [81920, 1536], P(('dp', 'ctx')), parts along dimension 0
- cont_value_grad: bfloat16 [81920, 1536], P(('dp', 'ctx')), parts along dimension 0
- prompt_key_grad: bfloat16 [65536, 1536], P(('dp', 'ctx')), parts along dimension 0
- prompt_value_grad: bfloat16 [65536, 1536], P(('dp', 'ctx')), parts along dimension 0
The draws below stay inside these ranges and needn't reach their ends.
There are 8 independent parts, one for each index of `dp`. The reference program is written for one: setup_inputs(seed, part) draws one part's arguments, and reference() takes and returns one part's arrays. A program takes and returns all parts, laid end to end along the dimension named above; each array names one. Nothing has to cross between parts.
Inputs may be any that keep to these rules, and one draw needn't show every extreme that they name: `prompt_links`: 1 where continuation block j reads prompt block j - d (column d), else 0; column 0 is always 1; no link points before block 0. `cont_start`: j or j - 1 for block j; a continuation is a run of 1 to 2 consecutive blocks. `valid_len`: 320 in every block but the last of its continuation.
All inputs are finite; a program needn't handle non-finite values.
Results may differ from the reference program's by a relative error of at most 0.0087.
Values may be sent and summed in bfloat16 or wider, within the bound.
A program may use at most 192 MiB of HBM per device.

```python
import jax
import jax.numpy as jnp
from jax import lax

HEADS = 24
HD = 64
D = 1536
CB = 320
PB = 256
REACH = 3
NBLK = 32
NC = 10240
NP = 8192


def layout(key):
    blocks = NC // CB
    coins = jax.random.randint(key, (blocks,), 0, 2)
    coins = coins.at[0].set(0).at[1].set(1)

    def step(prev_joined, coin):
        joined = coin * (1 - prev_joined)
        return (joined, joined)
    _, joined = lax.scan(step, jnp.int32(0), coins)
    return joined


def draw_cont_query(key, part):
    key = jax.random.fold_in(key, 11)
    return jnp.clip(jax.random.normal(key, (NC, D), jnp.float32), -6.0, 6.0).astype(jnp.bfloat16)


def draw_prompt_key(key, part):
    key = jax.random.fold_in(key, 13)
    return jnp.clip(jax.random.normal(key, (NP, D), jnp.float32), -6.0, 6.0).astype(jnp.bfloat16)


def draw_cont_start(key, part):
    joined = layout(key)
    blocks = jnp.arange(NC // CB, dtype=jnp.int32)
    return blocks - joined


def draw_valid_len(key, part):
    joined = layout(key)
    key = jax.random.fold_in(key, 5)
    following = jnp.concatenate([joined[1:], jnp.zeros((1,), jnp.int32)])
    lengths = jax.random.randint(key, (NC // CB,), CB // 4, CB + 1)
    return jnp.where(following == 0, lengths, CB).astype(jnp.int32)


def draw_prompt_links(key, part):
    key = jax.random.fold_in(key, 7)
    blocks = NC // CB
    coins = (jax.random.randint(key, (blocks, REACH), 0, 4) != 0).astype(jnp.int32)
    column = jnp.arange(REACH, dtype=jnp.int32)[None, :]
    rowpos = jnp.arange(blocks, dtype=jnp.int32)[:, None]
    links = jnp.where(column == 0, 1, coins)
    links = links.at[2, :].set(1)
    links = jnp.where(rowpos - column >= 0, links, 0)
    return links.astype(jnp.int32)


def steps_of(stream_key, extent, pieces, smallest, top_value):
    loudness, own = 1.0, jax.random.fold_in(stream_key, 6)
    for axis_at, parts in pieces:
        heights = jnp.exp(jax.random.uniform(jax.random.fold_in(own, axis_at), (parts,), jnp.float32, smallest / len(pieces), top_value / len(pieces)))
        loudness = loudness * jnp.repeat(heights, extent[axis_at] // parts).reshape([-1 if axis == axis_at else 1 for axis in range(len(extent))])
    return loudness


def scatter_about(key, extent, deviation, bound, cuts=(), kind=jnp.bfloat16):
    entries = deviation * jax.random.normal(key, extent, jnp.float32)
    if cuts:
        entries = entries * steps_of(key, extent, cuts, -0.22, 0.18)
    return jnp.clip(entries, -bound, bound).astype(kind)


def setup_inputs(seed: int = 0, part: int = 0) -> dict:
    key_of = jax.random.split(jax.random.key(seed), 10)
    own_keys = jax.random.split(jax.random.fold_in(key_of[9], part), 10)
    cont_query = draw_cont_query(jax.random.fold_in(jax.random.fold_in(key_of[9], part), 71), part)
    cont_key = scatter_about(own_keys[1], (NC, D), 1.0, 6.0, ((0, 32),))
    cont_value = scatter_about(own_keys[2], (NC, D), 1.0, 6.0, ((0, 32),))
    prompt_key = draw_prompt_key(jax.random.fold_in(jax.random.fold_in(key_of[9], part), 71), part)
    prompt_value = scatter_about(own_keys[4], (NP, D), 1.0, 6.0, ((0, 32),))
    out_grad = scatter_about(own_keys[5], (NC, D), 1.0, 6.0, ((0, 32),))
    prompt_links = draw_prompt_links(jax.random.fold_in(jax.random.fold_in(key_of[9], part), 71), part)
    cont_start = draw_cont_start(jax.random.fold_in(jax.random.fold_in(key_of[9], part), 71), part)
    valid_len = draw_valid_len(jax.random.fold_in(jax.random.fold_in(key_of[9], part), 71), part)
    return dict(cont_query=cont_query, cont_key=cont_key, cont_value=cont_value, prompt_key=prompt_key, prompt_value=prompt_value, out_grad=out_grad, prompt_links=prompt_links, cont_start=cont_start, valid_len=valid_len)


def heads_pass(queries, key_rows, value_rows, grad_rows, visible):
    scale = HD ** -0.5
    q_heads = queries.astype(jnp.float32).reshape(queries.shape[0], HEADS, HD)
    k_heads = key_rows.astype(jnp.float32).reshape(key_rows.shape[0], HEADS, HD)
    v_heads = value_rows.astype(jnp.float32).reshape(value_rows.shape[0], HEADS, HD)
    g_heads = grad_rows.astype(jnp.float32).reshape(grad_rows.shape[0], HEADS, HD)
    scores = jnp.einsum("qhd,khd->hqk", q_heads, k_heads) * scale
    scores = jnp.where(visible[None], scores, -1e30)
    top_score = jnp.max(scores, axis=-1, keepdims=True)
    expo = jnp.exp(scores - top_score)
    weights = expo / jnp.sum(expo, axis=-1, keepdims=True)
    weights_low = lax.optimization_barrier(weights.astype(jnp.bfloat16)).astype(jnp.float32)
    output = jnp.einsum("hqk,khd->qhd", weights_low, v_heads)
    dweights = jnp.einsum("qhd,khd->hqk", g_heads, v_heads)
    delta = jnp.sum(weights * dweights, axis=-1, keepdims=True)
    dscores = (weights * (dweights - delta) * scale).astype(jnp.bfloat16)
    dscores = lax.optimization_barrier(dscores).astype(jnp.float32)
    dquery = jnp.einsum("hqk,khd->qhd", dscores, k_heads)
    dkey = jnp.einsum("hqk,qhd->khd", dscores, q_heads)
    dvalue = jnp.einsum("hqk,qhd->khd", weights_low, g_heads)
    width = HEADS * HD
    return (output.reshape(-1, width), dquery.reshape(-1, width),
            dkey.reshape(-1, width), dvalue.reshape(-1, width))


def take_block(array, block, count):
    start = (jnp.maximum(block, 0) * count).astype(jnp.int32)
    return lax.dynamic_slice_in_dim(array, start, count, 0)


def add_block(accum, part, block, count):
    start = (jnp.maximum(block, 0) * count).astype(jnp.int32)
    current = lax.dynamic_slice_in_dim(accum, start, count, 0)
    return lax.dynamic_update_slice_in_dim(accum, current + part, start, 0)


def reference(cont_query, cont_key, cont_value, prompt_key, prompt_value, out_grad, prompt_links, cont_start, valid_len):
    width = HEADS * HD

    def one_block(carry, block):
        pk_grad, pv_grad, ck_grad, cv_grad = carry
        prompt_blocks = [block - shift_by for shift_by in range(REACH)]
        key_rows = jnp.concatenate([take_block(prompt_key, b, PB) for b in prompt_blocks]
                                   + [take_block(cont_key, block - 1, CB), take_block(cont_key, block, CB)], 0)
        value_rows = jnp.concatenate([take_block(prompt_value, b, PB) for b in prompt_blocks]
                                     + [take_block(cont_value, block - 1, CB), take_block(cont_value, block, CB)], 0)
        queries = take_block(cont_query, block, CB)
        links = prompt_links[block]
        prompt_cols = jnp.repeat(links > 0, PB, total_repeat_length=REACH * PB)
        prev_len = valid_len[jnp.maximum(block - 1, 0)]
        own_len = valid_len[block]
        prev_ok = cont_start[block] <= block - 1
        position = jnp.arange(CB, dtype=jnp.int32)
        prev_cols = prev_ok & (position < prev_len)
        own_cols = (position[None, :] <= position[:, None]) & (position[None, :] < own_len)
        visible = jnp.concatenate([jnp.broadcast_to(prompt_cols[None], (CB, REACH * PB)),
                                   jnp.broadcast_to(prev_cols[None], (CB, CB)), own_cols], 1)
        row_live = (position < own_len)[:, None]
        grad_in = jnp.where(row_live, take_block(out_grad, block, CB), jnp.zeros((), jnp.bfloat16)).astype(jnp.bfloat16)
        output, dquery, dkey, dvalue = heads_pass(queries, key_rows, value_rows, grad_in, visible)
        attended_rows = jnp.where(row_live, output, 0.0).astype(jnp.bfloat16)
        for shift_by in range(REACH):
            lower = shift_by * PB
            pk_grad = add_block(pk_grad, dkey[lower:lower + PB], prompt_blocks[shift_by], PB)
            pv_grad = add_block(pv_grad, dvalue[lower:lower + PB], prompt_blocks[shift_by], PB)
        lower = REACH * PB
        ck_grad = add_block(ck_grad, dkey[lower:lower + CB], block - 1, CB)
        cv_grad = add_block(cv_grad, dvalue[lower:lower + CB], block - 1, CB)
        ck_grad = add_block(ck_grad, dkey[lower + CB:], block, CB)
        cv_grad = add_block(cv_grad, dvalue[lower + CB:], block, CB)
        return (pk_grad, pv_grad, ck_grad, cv_grad), (attended_rows, dquery.astype(jnp.bfloat16))

    start_carry = (jnp.zeros((NP, width), jnp.float32), jnp.zeros((NP, width), jnp.float32),
                   jnp.zeros((NC, width), jnp.float32), jnp.zeros((NC, width), jnp.float32))
    totals, stacked = lax.scan(one_block, start_carry, jnp.arange(NBLK, dtype=jnp.int32))
    attended = stacked[0].reshape(NC, width)
    query_grad = stacked[1].reshape(NC, width)
    return (attended, query_grad, totals[2].astype(jnp.bfloat16), totals[3].astype(jnp.bfloat16),
            totals[0].astype(jnp.bfloat16), totals[1].astype(jnp.bfloat16))
```

```python
import functools

import jax
import jax.numpy as jnp
from jax import lax
from jax.experimental import pallas as pl
from jax.experimental.pallas import tpu as pltpu
from jax.sharding import PartitionSpec as P

HD = 64
PAIR = 2 * HD
AHEAD = 3
LAG = 3
LOG2E = 1.4426950408889634
F32 = jnp.float32
BF16 = jnp.bfloat16
MESH = pl.DeviceIdType.MESH


def mm(a, b):
    return lax.dot_general(a, b, (((1,), (0,)), ((), ())), preferred_element_type=F32)


def mm_t(a, b):
    return lax.dot_general(a, b, (((1,), (1,)), ((), ())), preferred_element_type=F32)


def kernel(
    chunks,
    length,
    q_ref,
    g_ref,
    ck_ref,
    cv_ref,
    pk_ref,
    pv_ref,
    links_ref,
    start_ref,
    valid_ref,
    o_ref,
    dq_ref,
    ckg_ref,
    cvg_ref,
    pkg_ref,
    pvg_ref,
    kv,
    bias,
    own,
    mid,
    send_near,
    send_far,
    got_near,
    got_far,
    got_sib,
    near_out,
    near_in,
    far_out,
    far_in,
    fwd_out,
    own_in,
    rnear_out,
    rnear_in,
    rfar_out,
    rfar_in,
    rsib_in,
):
    step = pl.program_id(0)
    cb = ck_ref.shape[0]
    pb = pk_ref.shape[0]
    both = cb + pb
    j = lax.axis_index("ctx")
    even = lax.rem(j, 2) == 0
    odd = lax.rem(j, 2) == 1
    nxt = lax.rem(j + 1, length)
    nxt2 = lax.rem(j + 2, length)
    prv = lax.rem(j + length - 1, length)
    prv2 = lax.rem(j + length - 2, length)

    def cols(c):
        return pl.ds(pl.multiple_of(c * PAIR, PAIR), PAIR)

    def remote(src, dst, out_sem, in_sem, to):
        return pltpu.make_async_remote_copy(
            src_ref=src,
            dst_ref=dst,
            send_sem=out_sem,
            recv_sem=in_sem,
            device_id={"ctx": to},
            device_id_type=MESH,
        )

    def wait_bytes(ref, sem):
        pltpu.make_async_copy(ref, ref, sem).wait()

    def near_rows(c):
        return kv.at[c, :, pl.ds(both, both)]

    def far_rows(c):
        return kv.at[c, :, pl.ds(2 * both, pb)]

    def send_inputs(c):
        for which, (cont, prompt) in enumerate(((ck_ref, pk_ref), (cv_ref, pv_ref))):
            cont_c, prompt_c = cont.at[:, cols(c)], prompt.at[:, cols(c)]
            remote(
                prompt_c,
                kv.at[c, which, pl.ds(both + cb, pb)],
                near_out.at[c],
                near_in.at[c],
                nxt,
            ).start()
            remote(
                cont_c, kv.at[c, which, pl.ds(both, cb)], near_out.at[c], near_in.at[c], nxt
            ).start()

            @pl.when(even)
            def _():
                remote(
                    prompt_c,
                    kv.at[c, which, pl.ds(2 * both, pb)],
                    far_out.at[c],
                    far_in.at[c],
                    nxt2,
                ).start()

            pltpu.make_async_copy(cont_c, kv.at[c, which, pl.ds(0, cb)], own_in.at[c]).start()
            pltpu.make_async_copy(prompt_c, kv.at[c, which, pl.ds(cb, pb)], own_in.at[c]).start()

    own_len = valid_ref[j]
    row = lax.broadcasted_iota(jnp.int32, (cb, 1), 0)
    live = row < own_len

    @pl.when(step == 0)
    def _():
        barrier = pltpu.get_barrier_semaphore()
        for other in (nxt, nxt2, prv, prv2):
            pl.semaphore_signal(barrier, inc=1, device_id={"ctx": other}, device_id_type=MESH)
        pl.semaphore_wait(barrier, 4)
        for c in range(AHEAD):
            send_inputs(c)
        prev_len = valid_ref[jnp.maximum(j - 1, 0)]
        near_cont = jnp.where(start_ref[0] <= j - 1, prev_len, 0)
        limits = [jnp.where(links_ref[0, d] > 0, pb, 0) for d in range(3)]
        key = lax.broadcasted_iota(jnp.int32, (cb, 2 * both + pb), 1)
        query = lax.broadcasted_iota(jnp.int32, (cb, 2 * both + pb), 0)
        own_limit = jnp.minimum(query, own_len - 1)
        limit = jnp.where(
            key < cb,
            own_limit + 1,
            jnp.where(
                key < both,
                limits[0] + cb,
                jnp.where(
                    key < both + cb,
                    near_cont + both,
                    jnp.where(
                        key < 2 * both, limits[1] + (both + cb), limits[2] + 2 * both
                    ),
                ),
            ),
        )
        bias[...] = jnp.where(key < limit, 0.0, -1e30)

    @pl.when(step + AHEAD < chunks)
    def _():
        @pl.when(step > 0)
        def _():
            send_inputs(step + AHEAD - 1)

    @pl.when(step + AHEAD == chunks)
    def _():
        send_inputs(step + AHEAD - 1)

    @pl.when(step < chunks)
    def _():
        c = step
        wait_bytes(near_rows(c), near_in.at[c])

        @pl.when(even)
        def _():
            for which in range(2):
                remote(
                    kv.at[c, which, pl.ds(both + cb, pb)],
                    kv.at[c, which, pl.ds(2 * both, pb)],
                    fwd_out.at[c],
                    far_in.at[c],
                    nxt,
                ).start()

    def return_near(c):
        remote(
            send_near.at[c], got_near.at[c], rnear_out.at[c], rnear_in.at[c], prv
        ).start()

    @pl.when((step > 0) & (step <= chunks) & even)
    def _():
        c = step - 1
        wait_bytes(got_sib.at[c], rsib_in.at[c])
        send_near[c, :, cb:, :] = (mid[...] + got_sib[c].astype(F32)).astype(BF16)
        return_near(c)

    @pl.when(step < chunks)
    def _():
        c = step
        wait_bytes(kv.at[c, :, pl.ds(0, both)], own_in.at[c])
        wait_bytes(far_rows(c), far_in.at[c])
        first = lax.broadcasted_iota(jnp.int32, (cb, PAIR), 1) < HD
        k = kv[c, 0]
        v = kv[c, 1]
        q = q_ref[...] * jnp.asarray(HD ** (-0.5), BF16)
        zero = jnp.zeros((), BF16)
        qs = jnp.concatenate([jnp.where(first, q, zero), jnp.where(first, zero, q)], 0)
        b = bias[...]
        s = mm_t(qs, k) + jnp.concatenate([b, b], 0)
        top = jnp.max(s, axis=1, keepdims=True)
        e = jnp.exp2((s - top) * LOG2E)
        inv = 1.0 / jnp.sum(e, axis=1, keepdims=True)
        e = e.astype(BF16)
        o = mm(e, v) * inv
        o_pair = jnp.where(first, o[:cb], o[cb:])
        o_ref[...] = jnp.where(live, o_pair, 0.0).astype(BF16)
        g = jnp.where(live, g_ref[...].astype(F32), 0.0)
        gs = jnp.concatenate([jnp.where(first, g, 0.0), jnp.where(first, 0.0, g)], 0)
        gs = (gs * inv).astype(BF16)
        delta = jnp.sum(gs.astype(F32) * o, axis=1, keepdims=True)
        dp = mm_t(gs, v)
        ds = (e.astype(F32) * (dp - delta)).astype(BF16)
        dq = mm(ds, k) * (HD ** (-0.5))
        dq_ref[...] = jnp.where(first, dq[:cb], dq[cb:]).astype(BF16)
        grads = (mm(qs.T, ds).T, mm(gs.T, e).T)
        for which in range(2):
            own[c, which] = grads[which][:both]
            send_near[c, which, :cb, :] = grads[which][both : both + cb].astype(BF16)
            mid[which] = grads[which][both + cb : 2 * both]
            send_far[c, which] = grads[which][2 * both :].astype(BF16)

        @pl.when(odd)
        def _():
            for which in range(2):
                send_near[c, which, cb:, :] = mid[which].astype(BF16)
            remote(
                send_far.at[c], got_sib.at[c], rfar_out.at[c], rsib_in.at[c], prv
            ).start()
            return_near(c)

        @pl.when(even)
        def _():
            remote(
                send_far.at[c], got_far.at[c], rfar_out.at[c], rfar_in.at[c], prv2
            ).start()

    @pl.when(step >= LAG)
    def _():
        c = step - LAG
        wait_bytes(got_near.at[c], rnear_in.at[c])

        @pl.when(even)
        def _():
            wait_bytes(got_far.at[c], rfar_in.at[c])
            own[c, :, cb:, :] += got_far[c].astype(F32)

        for which, (cont, prompt) in enumerate(((ckg_ref, pkg_ref), (cvg_ref, pvg_ref))):
            total = own[c, which] + got_near[c, which].astype(F32)
            cont[...] = total[:cb].astype(BF16)
            prompt[...] = total[cb:].astype(BF16)

        wait_bytes(near_rows(c), near_out.at[c])
        wait_bytes(send_near.at[c], rnear_out.at[c])
        wait_bytes(send_far.at[c], rfar_out.at[c])

        @pl.when(even)
        def _():
            wait_bytes(far_rows(c), far_out.at[c])
            wait_bytes(far_rows(c), fwd_out.at[c])


def per_device(*args):
    q, ck, cv, pk, pv, g, links, start, valid = args
    cb, width = q.shape
    pb = pk.shape[0]
    chunks = width // PAIR
    length = lax.axis_size("ctx")
    keys = 2 * cb + 3 * pb
    both = cb + pb

    def early(rows):
        return pl.BlockSpec((rows, PAIR), lambda c: (0, jnp.minimum(c, chunks - 1)))

    def late(rows):
        return pl.BlockSpec((rows, PAIR), lambda c: (0, jnp.maximum(c - LAG, 0)))

    anywhere = pl.BlockSpec(memory_space=pl.ANY)
    scalars = pl.BlockSpec(memory_space=pltpu.SMEM)
    wide = jax.ShapeDtypeStruct((cb, width), BF16)
    short = jax.ShapeDtypeStruct((pb, width), BF16)
    work = 12 * cb * keys * width
    return pl.pallas_call(
        functools.partial(kernel, chunks, length),
        grid=(chunks + LAG,),
        in_specs=[early(cb), early(cb)] + [anywhere] * 4 + [scalars] * 3,
        out_specs=[early(cb), early(cb), late(cb), late(cb), late(pb), late(pb)],
        out_shape=[wide, wide, wide, wide, short, short],
        scratch_shapes=[
            pltpu.VMEM((chunks, 2, keys, PAIR), BF16),
            pltpu.VMEM((cb, keys), F32),
            pltpu.VMEM((chunks, 2, both, PAIR), F32),
            pltpu.VMEM((2, pb, PAIR), F32),
            pltpu.VMEM((chunks, 2, both, PAIR), BF16),
            pltpu.VMEM((chunks, 2, pb, PAIR), BF16),
            pltpu.VMEM((chunks, 2, both, PAIR), BF16),
            pltpu.VMEM((chunks, 2, pb, PAIR), BF16),
            pltpu.VMEM((chunks, 2, pb, PAIR), BF16),
        ]
        + [pltpu.SemaphoreType.DMA((chunks,))] * 11,
        compiler_params=pltpu.CompilerParams(
            collective_id=0, has_side_effects=True, vmem_limit_bytes=58 * 2**20
        ),
        cost_estimate=pl.CostEstimate(
            flops=work, bytes_accessed=12 * 2 * cb * width, transcendentals=cb * keys * width // HD
        ),
    )(q, g, ck, cv, pk, pv, links, start, valid)


def solution(mesh):
    rows = P(("dp", "ctx"), None)
    return jax.shard_map(
        per_device,
        mesh=mesh,
        in_specs=(rows,) * 7 + (P(("dp", "ctx")), P("dp")),
        out_specs=(rows,) * 6,
        check_vma=False,
    )
```

```python
import functools

import jax
import jax.numpy as jnp
from jax import lax
from jax.experimental import pallas as pl
from jax.experimental.pallas import tpu as pltpu
from jax.sharding import PartitionSpec as P

HD = 64
PAIR = 2 * HD
AHEAD = 4
LAG = 5
SCALE = HD ** (-0.5)
LOG2E = 1.4426950408889634
F32 = jnp.float32
BF16 = jnp.bfloat16
MESH = pl.DeviceIdType.MESH


def mm(a, b):
    return lax.dot_general(a, b, (((1,), (0,)), ((), ())), preferred_element_type=F32)


def mm_t(a, b):
    return lax.dot_general(a, b, (((1,), (1,)), ((), ())), preferred_element_type=F32)


def stacked(x):
    first = lax.broadcasted_iota(jnp.int32, x.shape, 1) < HD
    zero = jnp.zeros((), x.dtype)
    return jnp.concatenate([jnp.where(first, x, zero), jnp.where(first, zero, x)], 0)


def folded(x):
    half = x.shape[0] // 2
    first = lax.broadcasted_iota(jnp.int32, (half, PAIR), 1) < HD
    return jnp.where(first, x[:half], x[half:])


def as_rows(a, b):
    lane = lax.broadcasted_iota(jnp.int32, (a.shape[0], PAIR), 1)
    return jnp.where(lane == 0, a, jnp.where(lane == 1, b, 0.0)).T[:2]


def as_columns(rows):
    filled = jnp.concatenate([rows, jnp.zeros((PAIR - 2, rows.shape[1]), F32)], 0).T
    return filled[:, 0:1], filled[:, 1:2]


def softmax_parts(s, v):
    top = jnp.max(s, axis=1, keepdims=True)
    e = jnp.exp2((s - top) * LOG2E)
    total = jnp.sum(e, axis=1, keepdims=True)
    e = e.astype(BF16)
    out = mm(e, v) * (1.0 / total)
    return top, total, e, out


def gradients(e, qs, gs, k, v, delta, factor):
    ds = (e.astype(F32) * (mm_t(gs, v) - delta)).astype(BF16)
    dq = folded(mm(ds, k) * (factor * SCALE))
    dk = mm((qs.astype(F32) * factor).astype(BF16).T, ds).T
    dv = mm((gs.astype(F32) * factor).astype(BF16).T, e).T
    return dq, (dk, dv)


def kernel(
    chunks,
    length,
    q_ref,
    g_ref,
    ck_ref,
    cv_ref,
    pk_ref,
    pv_ref,
    links_ref,
    start_ref,
    valid_ref,
    o_ref,
    dq_ref,
    ckg_ref,
    cvg_ref,
    pkg_ref,
    pvg_ref,
    kv,
    mine,
    theirs,
    bias,
    row_bias,
    their_bias,
    exps,
    sums,
    own,
    own_dq,
    part_o,
    got_o,
    part_s,
    got_s,
    back_s,
    got_back,
    part_dq,
    got_dq,
    sib_g,
    got_sib,
    far_g,
    got_far,
    out_o,
    out_dq,
    out_g,
    kv_in,
    q_in,
    sib_out,
    sib_in,
    far_out,
    far_in,
    qg_out,
    qg_in,
    o_out,
    o_in,
    s_out,
    s_in,
    b_out,
    b_in,
    dq_out,
    dq_in,
    sg_out,
    sg_in,
    fg_out,
    fg_in,
    res_o,
    res_dq,
    res_g,
    rb_out,
    rb_in,
):
    step = pl.program_id(0)
    cb = ck_ref.shape[0]
    pb = pk_ref.shape[0]
    both = cb + pb
    j = lax.axis_index("ctx")
    parity = lax.rem(j, 2)
    even = parity == 0
    odd = parity == 1
    sib = j + 1 - 2 * parity
    nxt = lax.rem(j + 2, length)
    prv = lax.rem(j + length - 2, length)
    slots = own.shape[0]
    e_slots = exps.shape[0]

    def cols(c):
        return pl.ds(pl.multiple_of(c * PAIR, PAIR), PAIR)

    def send(src, dst, out_sem, in_sem, to):
        pltpu.make_async_remote_copy(
            src_ref=src,
            dst_ref=dst,
            send_sem=out_sem,
            recv_sem=in_sem,
            device_id={"ctx": to},
            device_id_type=MESH,
        ).start()

    def wait_bytes(ref, sem):
        pltpu.make_async_copy(ref, ref, sem).wait()

    def own_rows(c):
        return kv.at[c, :, pl.ds(0, both)]

    def sib_rows(c):
        return kv.at[c, :, pl.ds(both, both)]

    def far_rows(c):
        return kv.at[c, :, pl.ds(2 * both, pb)]

    def send_inputs(c):
        @pl.when(even)
        def _():
            send(q_ref.at[:, cols(c)], theirs.at[c, 0], qg_out.at[c], qg_in.at[c], prv)
            send(g_ref.at[:, cols(c)], theirs.at[c, 1], qg_out.at[c], qg_in.at[c], prv)

        @pl.when(odd)
        def _():
            for which, prompt in enumerate((pk_ref, pv_ref)):
                send(
                    prompt.at[:, cols(c)],
                    kv.at[c, which, pl.ds(2 * both, pb)],
                    far_out.at[c],
                    far_in.at[c],
                    nxt,
                )

        for which, (cont, prompt) in enumerate(((ck_ref, pk_ref), (cv_ref, pv_ref))):
            cont_c, prompt_c = cont.at[:, cols(c)], prompt.at[:, cols(c)]
            send(
                prompt_c, kv.at[c, which, pl.ds(both, pb)], sib_out.at[c], sib_in.at[c], sib
            )
            send(
                cont_c,
                kv.at[c, which, pl.ds(both + pb, cb)],
                sib_out.at[c],
                sib_in.at[c],
                sib,
            )
            pltpu.make_async_copy(cont_c, kv.at[c, which, pl.ds(0, cb)], kv_in.at[c]).start()
            pltpu.make_async_copy(prompt_c, kv.at[c, which, pl.ds(cb, pb)], kv_in.at[c]).start()
        pltpu.make_async_copy(q_ref.at[:, cols(c)], mine.at[c, 0], q_in.at[c]).start()
        pltpu.make_async_copy(g_ref.at[:, cols(c)], mine.at[c, 1], q_in.at[c]).start()

    def rows_of(ref, c, block):
        live = lax.broadcasted_iota(jnp.int32, (cb, 1), 0) < valid_ref[block]
        qs = stacked(ref[c, 0] * jnp.asarray(SCALE, BF16))
        gs = stacked(jnp.where(live, ref[c, 1].astype(F32), 0.0)).astype(BF16)
        return live, qs, gs

    def put_o(c, value):
        out_o[c] = value.astype(BF16)
        pltpu.make_async_copy(out_o.at[c], o_ref.at[:, cols(c)], res_o.at[c]).start()

    def put_dq(c, value):
        out_dq[c] = value.astype(BF16)
        pltpu.make_async_copy(out_dq.at[c], dq_ref.at[:, cols(c)], res_dq.at[c]).start()

    @pl.when(step == 0)
    def _():
        barrier = pltpu.get_barrier_semaphore()
        for other in (sib, nxt, prv):
            pl.semaphore_signal(barrier, inc=1, device_id={"ctx": other}, device_id_type=MESH)
        pl.semaphore_wait(barrier, 3)
        for c in range(AHEAD):
            send_inputs(c)
        near_cont = jnp.where(
            start_ref[0] <= j - 1, valid_ref[jnp.maximum(j - 1, 0)], 0
        )
        own_len = valid_ref[j]
        limits = [jnp.where(links_ref[0, d] > 0, pb, 0) for d in range(3)]
        far_key = lax.broadcasted_iota(jnp.int32, row_bias.shape, 1)
        far_limit = jnp.where(
            far_key < pb,
            limits[2],
            jnp.where(far_key < 2 * pb, limits[1] + pb, near_cont + 2 * pb),
        )
        row_bias[...] = jnp.where(far_key < far_limit, 0.0, -1e30)

        @pl.when(even)
        def _():
            send(row_bias, their_bias, rb_out, rb_in, prv)

        key = lax.broadcasted_iota(jnp.int32, (cb, 2 * both + pb), 1)
        query = lax.broadcasted_iota(jnp.int32, (cb, 2 * both + pb), 0)
        limit = jnp.where(
            key < cb,
            jnp.minimum(query, own_len - 1) + 1,
            jnp.where(
                key < both,
                limits[0] + cb,
                jnp.where(
                    key < both + pb,
                    limits[1] + both,
                    jnp.where(
                        key < 2 * both, near_cont + (both + pb), limits[2] + 2 * both
                    ),
                ),
            ),
        )
        bias[...] = jnp.where(key < limit, 0.0, -1e30)

        @pl.when(even)
        def _():
            wait_bytes(their_bias, rb_in)

    @pl.when((step > 0) & (step + AHEAD <= chunks))
    def _():
        send_inputs(step + AHEAD - 1)

    @pl.when((step < chunks) & odd)
    def _():
        c = step
        wait_bytes(own_rows(c), kv_in.at[c])
        wait_bytes(mine.at[c], q_in.at[c])
        wait_bytes(sib_rows(c), sib_in.at[c])
        wait_bytes(far_rows(c), far_in.at[c])
        live, qs, gs = rows_of(mine, c, j)
        k = kv[c, 0]
        v = kv[c, 1]
        b = bias[...]
        s = mm_t(qs, k) + jnp.concatenate([b, b], 0)
        top, total, e, out = softmax_parts(s, v)
        put_o(c, jnp.where(live, folded(out), 0.0))
        delta = jnp.sum(gs.astype(F32) * out, axis=1, keepdims=True)
        dq, grads = gradients(e, qs, gs, k, v, delta, 1.0 / total)
        put_dq(c, dq)
        for which in range(2):
            own[lax.rem(c, slots), which] = grads[which][:both]
            sib_g[c, which] = grads[which][both : 2 * both].astype(BF16)
            far_g[c, which] = grads[which][2 * both :].astype(BF16)
        send(far_g.at[c], got_far.at[c], fg_out.at[c], fg_in.at[c], prv)
        send(sib_g.at[c], got_sib.at[c], sg_out.at[c], sg_in.at[c], sib)

    @pl.when((step < chunks) & even)
    def _():
        c = step
        wait_bytes(own_rows(c), kv_in.at[c])
        wait_bytes(mine.at[c], q_in.at[c])
        wait_bytes(sib_rows(c), sib_in.at[c])
        wait_bytes(theirs.at[c], qg_in.at[c])
        _, qs, gs = rows_of(theirs, c, nxt)
        k = kv[c, 0, cb : 2 * both]
        v = kv[c, 1, cb : 2 * both]
        s = mm_t(qs, k) + their_bias[0:1, :]
        top, total, e, out = softmax_parts(s, v)
        part_o[c] = folded(out).astype(BF16)
        delta = jnp.sum(gs.astype(F32) * out, axis=1, keepdims=True)
        part_s[c] = as_rows((top + jnp.log(total)) * LOG2E, delta)
        send(part_s.at[c], got_s.at[c], s_out.at[c], s_in.at[c], nxt)
        send(part_o.at[c], got_o.at[c], o_out.at[c], o_in.at[c], nxt)
        exps[lax.rem(c, e_slots)] = e
        sums[lax.rem(c, e_slots)] = total

    @pl.when((step >= 1) & (step <= chunks) & even)
    def _():
        c = step - 1
        live, qs, gs = rows_of(mine, c, j)
        k = kv[c, 0, :both]
        v = kv[c, 1, :both]
        b = bias[:, :both]
        s = mm_t(qs, k) + jnp.concatenate([b, b], 0)
        top, total, e, out = softmax_parts(s, v)
        delta = jnp.sum(gs.astype(F32) * out, axis=1, keepdims=True)
        level = (top + jnp.log(total)) * LOG2E
        wait_bytes(got_s.at[c], s_in.at[c])
        far_level, far_delta = as_columns(got_s[c])
        high = jnp.maximum(level, far_level)
        mix = high + jnp.log(jnp.exp2(level - high) + jnp.exp2(far_level - high)) * LOG2E
        share = jnp.exp2(level - mix)
        far_share = jnp.exp2(far_level - mix)
        delta = share * delta + far_share * far_delta
        back_s[c] = as_rows(far_share, delta)
        send(back_s.at[c], got_back.at[c], b_out.at[c], b_in.at[c], prv)
        wait_bytes(got_o.at[c], o_in.at[c])
        spread = folded(jnp.broadcast_to(far_share, (2 * cb, PAIR)))
        mixed = folded(out * share) + spread * got_o[c].astype(F32)
        put_o(c, jnp.where(live, mixed, 0.0))
        dq, grads = gradients(e, qs, gs, k, v, delta, share / total)
        own_dq[lax.rem(c, slots)] = dq
        for which in range(2):
            own[lax.rem(c, slots), which] = grads[which]

    @pl.when((step >= 2) & (step <= chunks + 1) & even)
    def _():
        c = step - 2
        _, qs, gs = rows_of(theirs, c, nxt)
        k = kv[c, 0, cb : 2 * both]
        v = kv[c, 1, cb : 2 * both]
        wait_bytes(got_back.at[c], b_in.at[c])
        share, delta = as_columns(got_back[c])
        e = exps[lax.rem(c, e_slots)]
        dq, grads = gradients(e, qs, gs, k, v, delta, share / sums[lax.rem(c, e_slots)])
        part_dq[c] = dq.astype(BF16)
        send(part_dq.at[c], got_dq.at[c], dq_out.at[c], dq_in.at[c], nxt)
        for which in range(2):
            own[lax.rem(c, slots), which, cb:, :] += grads[which][:pb]
            sib_g[c, which] = grads[which][pb:].astype(BF16)
        send(sib_g.at[c], got_sib.at[c], sg_out.at[c], sg_in.at[c], sib)

    @pl.when(step >= LAG)
    def _():
        c = step - LAG
        slot = lax.rem(c, slots)

        @pl.when(odd)
        def _():
            wait_bytes(got_far.at[c], fg_in.at[c])
            own[slot, :, cb:, :] += got_far[c].astype(F32)

        @pl.when(even)
        def _():
            wait_bytes(got_dq.at[c], dq_in.at[c])
            put_dq(c, own_dq[slot] + got_dq[c].astype(F32))

        wait_bytes(got_sib.at[c], sg_in.at[c])
        for which, (cont, prompt) in enumerate(((ckg_ref, pkg_ref), (cvg_ref, pvg_ref))):
            out_g[c, which, :cb, :] = (
                own[slot, which, :cb, :] + got_sib[c, which, pb:, :].astype(F32)
            ).astype(BF16)
            out_g[c, which, cb:, :] = (
                own[slot, which, cb:, :] + got_sib[c, which, :pb, :].astype(F32)
            ).astype(BF16)
            pltpu.make_async_copy(
                out_g.at[c, which, pl.ds(0, cb)], cont.at[:, cols(c)], res_g.at[c]
            ).start()
            pltpu.make_async_copy(
                out_g.at[c, which, pl.ds(cb, pb)], prompt.at[:, cols(c)], res_g.at[c]
            ).start()

    @pl.when(step == chunks + LAG - 1)
    def _():
        def finish(c, carry):
            wait_bytes(sib_rows(c), sib_out.at[c])
            wait_bytes(sib_g.at[c], sg_out.at[c])
            wait_bytes(out_o.at[c], res_o.at[c])
            wait_bytes(out_dq.at[c], res_dq.at[c])
            wait_bytes(out_g.at[c], res_g.at[c])

            @pl.when(even)
            def _():
                wait_bytes(theirs.at[c], qg_out.at[c])
                wait_bytes(part_o.at[c], o_out.at[c])
                wait_bytes(part_s.at[c], s_out.at[c])
                wait_bytes(back_s.at[c], b_out.at[c])
                wait_bytes(part_dq.at[c], dq_out.at[c])

            @pl.when(odd)
            def _():
                wait_bytes(far_rows(c), far_out.at[c])
                wait_bytes(far_g.at[c], fg_out.at[c])

            return carry

        lax.fori_loop(0, chunks, finish, 0)

        @pl.when(even)
        def _():
            wait_bytes(row_bias, rb_out)


def per_device(*args):
    q, ck, cv, pk, pv, g, links, start, valid = args
    cb, width = q.shape
    pb = pk.shape[0]
    chunks = width // PAIR
    length = lax.axis_size("ctx")
    keys = 2 * cb + 3 * pb
    both = cb + pb
    far_keys = cb + 2 * pb
    anywhere = pl.BlockSpec(memory_space=pl.ANY)
    scalars = pl.BlockSpec(memory_space=pltpu.SMEM)
    wide = jax.ShapeDtypeStruct((cb, width), BF16)
    short = jax.ShapeDtypeStruct((pb, width), BF16)
    work = 12 * cb * keys * width
    rows = pltpu.VMEM((chunks, cb, PAIR), BF16)
    stats = pltpu.VMEM((chunks, 2, 2 * cb), F32)
    pair_rows = pltpu.VMEM((chunks, 2, cb, PAIR), BF16)
    sib_grad = pltpu.VMEM((chunks, 2, both, PAIR), BF16)
    far_grad = pltpu.VMEM((chunks, 2, pb, PAIR), BF16)
    return pl.pallas_call(
        functools.partial(kernel, chunks, length),
        grid=(chunks + LAG,),
        in_specs=[anywhere] * 6 + [scalars] * 3,
        out_specs=[anywhere] * 6,
        out_shape=[wide, wide, wide, wide, short, short],
        scratch_shapes=[
            pltpu.VMEM((chunks, 2, keys, PAIR), BF16),
            pair_rows,
            pair_rows,
            pltpu.VMEM((cb, keys), F32),
            pltpu.VMEM((8, far_keys), F32),
            pltpu.VMEM((8, far_keys), F32),
            pltpu.VMEM((3, 2 * cb, far_keys), BF16),
            pltpu.VMEM((3, 2 * cb, 1), F32),
            pltpu.VMEM((LAG + 1, 2, both, PAIR), F32),
            pltpu.VMEM((LAG + 1, cb, PAIR), F32),
            rows,
            rows,
            stats,
            stats,
            stats,
            stats,
            rows,
            rows,
            sib_grad,
            sib_grad,
            far_grad,
            far_grad,
            rows,
            rows,
            sib_grad,
        ]
        + [pltpu.SemaphoreType.DMA((chunks,))] * 23
        + [pltpu.SemaphoreType.DMA] * 2,
        compiler_params=pltpu.CompilerParams(
            collective_id=0, has_side_effects=True, vmem_limit_bytes=60 * 2**20
        ),
        cost_estimate=pl.CostEstimate(
            flops=work, bytes_accessed=12 * 2 * cb * width, transcendentals=cb * keys * width // HD
        ),
    )(q, g, ck, cv, pk, pv, links, start, valid)


def solution(mesh):
    rows = P(("dp", "ctx"), None)
    return jax.shard_map(
        per_device,
        mesh=mesh,
        in_specs=(rows,) * 7 + (P(("dp", "ctx")), P("dp")),
        out_specs=(rows,) * 6,
        check_vma=False,
    )
```

```python
import functools

import jax
import jax.numpy as jnp
from jax import lax
from jax.experimental import pallas as pl
from jax.experimental.pallas import tpu as pltpu
from jax.sharding import PartitionSpec as P

HD = 64
PAIR = 2 * HD
QUERY_AHEAD = 3
FAR_AHEAD = 3
SIB_AHEAD = 3
MERGE_LAG = 2
BACK_LAG = 4
LAG = 6
SCALE = HD ** (-0.5)
LOG2E = 1.4426950408889634
F32 = jnp.float32
BF16 = jnp.bfloat16
MESH = pl.DeviceIdType.MESH


def mm(a, b):
    return lax.dot_general(a, b, (((1,), (0,)), ((), ())), preferred_element_type=F32)


def mm_t(a, b):
    return lax.dot_general(a, b, (((1,), (1,)), ((), ())), preferred_element_type=F32)


def stacked(x):
    first = lax.broadcasted_iota(jnp.int32, x.shape, 1) < HD
    zero = jnp.zeros((), x.dtype)
    return jnp.concatenate([jnp.where(first, x, zero), jnp.where(first, zero, x)], 0)


def folded(x):
    half = x.shape[0] // 2
    first = lax.broadcasted_iota(jnp.int32, (half, PAIR), 1) < HD
    return jnp.where(first, x[:half], x[half:])


def as_rows(a, b, c):
    lane = lax.broadcasted_iota(jnp.int32, (a.shape[0], PAIR), 1)
    turned = jnp.where(lane == 0, a, jnp.where(lane == 1, b, c)).T
    return turned[0:1], turned[1:2], turned[2:3]


def spread(row):
    return jnp.broadcast_to(row, (PAIR, row.shape[1])).T


def repeated(x, count):
    return jnp.concatenate([x] * (-(-count // PAIR)), 1)[:, :count]


def softmax_parts(s, v):
    top = jnp.max(s, axis=1, keepdims=True)
    e = jnp.exp2((s - top) * LOG2E)
    total = jnp.sum(e, axis=1, keepdims=True)
    e = e.astype(BF16)
    return top, total, e, mm(e, v)


def row_dot(gs, out):
    return jnp.sum(gs.astype(F32) * out, axis=1, keepdims=True)


def gradients(e, qs, gs, k, v, delta, factor):
    shifted = mm_t(gs, v) - repeated(delta, k.shape[0])
    ds = (e.astype(F32) * shifted).astype(BF16)
    dq = folded(mm(ds, k) * (factor * SCALE))
    dk = mm((qs.astype(F32) * factor).astype(BF16).T, ds).T
    dv = mm((gs.astype(F32) * factor).astype(BF16).T, e).T
    return dq, (dk, dv)


def kernel(
    chunks,
    length,
    q_ref,
    g_ref,
    ck_ref,
    cv_ref,
    pk_ref,
    pv_ref,
    links_ref,
    start_ref,
    valid_ref,
    o_ref,
    dq_ref,
    ckg_ref,
    cvg_ref,
    pkg_ref,
    pvg_ref,
    kv,
    mine,
    theirs,
    bias,
    row_bias,
    their_bias,
    exps,
    sums,
    own,
    own_dq,
    part_o,
    got_o,
    part_s,
    got_s,
    back_s,
    got_back,
    part_dq,
    got_dq,
    sib_g,
    got_sib,
    far_g,
    got_far,
    out_o,
    out_dq,
    out_g,
    kv_in,
    q_in,
    sib_out,
    sib_in,
    far_out,
    far_in,
    qg_out,
    qg_in,
    o_out,
    o_in,
    s_out,
    s_in,
    b_out,
    b_in,
    dq_out,
    dq_in,
    sg_out,
    sg_in,
    fg_out,
    fg_in,
    res_o,
    res_dq,
    res_g,
    rb_out,
    rb_in,
):
    step = pl.program_id(0)
    cb = ck_ref.shape[0]
    pb = pk_ref.shape[0]
    both = cb + pb
    j = lax.axis_index("ctx")
    parity = lax.rem(j, 2)
    even = parity == 0
    odd = parity == 1
    sib = j + 1 - 2 * parity
    nxt = lax.rem(j + 2, length)
    prv = lax.rem(j + length - 2, length)
    has_next = j + 2 < length
    has_prev = j >= 2
    slots = own.shape[0]
    e_slots = exps.shape[0]

    def cols(c):
        return pl.ds(pl.multiple_of(c * PAIR, PAIR), PAIR)

    def send(src, dst, out_sem, in_sem, to):
        pltpu.make_async_remote_copy(
            src_ref=src,
            dst_ref=dst,
            send_sem=out_sem,
            recv_sem=in_sem,
            device_id={"ctx": to},
            device_id_type=MESH,
        ).start()

    def wait_bytes(ref, sem):
        pltpu.make_async_copy(ref, ref, sem).wait()

    def own_rows(c):
        return kv.at[c, :, pl.ds(0, both)]

    def sib_rows(c):
        return kv.at[c, :, pl.ds(both, both)]

    def far_rows(c):
        return kv.at[c, :, pl.ds(2 * both, pb)]

    def send_far(c):
        for which, prompt in enumerate((pk_ref, pv_ref)):
            send(
                prompt.at[:, cols(c)],
                kv.at[c, which, pl.ds(2 * both, pb)],
                far_out.at[c],
                far_in.at[c],
                nxt,
            )

    def send_queries(c):
        send(q_ref.at[:, cols(c)], theirs.at[c, 0], qg_out.at[c], qg_in.at[c], prv)
        send(g_ref.at[:, cols(c)], theirs.at[c, 1], qg_out.at[c], qg_in.at[c], prv)

    def send_sib(c):
        for which, (cont, prompt) in enumerate(((ck_ref, pk_ref), (cv_ref, pv_ref))):
            cont_c, prompt_c = cont.at[:, cols(c)], prompt.at[:, cols(c)]
            send(
                prompt_c, kv.at[c, which, pl.ds(both, pb)], sib_out.at[c], sib_in.at[c], sib
            )
            send(
                cont_c,
                kv.at[c, which, pl.ds(both + pb, cb)],
                sib_out.at[c],
                sib_in.at[c],
                sib,
            )
            pltpu.make_async_copy(cont_c, kv.at[c, which, pl.ds(0, cb)], kv_in.at[c]).start()
            pltpu.make_async_copy(prompt_c, kv.at[c, which, pl.ds(cb, pb)], kv_in.at[c]).start()
        pltpu.make_async_copy(q_ref.at[:, cols(c)], mine.at[c, 0], q_in.at[c]).start()
        pltpu.make_async_copy(g_ref.at[:, cols(c)], mine.at[c, 1], q_in.at[c]).start()

    def rows_of(ref, c, block):
        live = lax.broadcasted_iota(jnp.int32, (cb, 1), 0) < valid_ref[block]
        qs = stacked(ref[c, 0] * jnp.asarray(SCALE, BF16))
        gs = stacked(jnp.where(live, ref[c, 1].astype(F32), 0.0)).astype(BF16)
        return live, qs, gs

    def put_o(c, value):
        out_o[c] = value.astype(BF16)
        pltpu.make_async_copy(out_o.at[c], o_ref.at[:, cols(c)], res_o.at[c]).start()

    def put_dq(c, value):
        out_dq[c] = value.astype(BF16)
        pltpu.make_async_copy(out_dq.at[c], dq_ref.at[:, cols(c)], res_dq.at[c]).start()

    @pl.when(step == 0)
    def _():
        barrier = pltpu.get_barrier_semaphore()

        def greet(other):
            pl.semaphore_signal(barrier, inc=1, device_id={"ctx": other}, device_id_type=MESH)

        greet(sib)

        @pl.when(has_next)
        def _():
            greet(nxt)

        @pl.when(has_prev)
        def _():
            greet(prv)

        @pl.when(has_next & has_prev)
        def _():
            pl.semaphore_wait(barrier, 3)

        @pl.when(jnp.logical_not(has_next & has_prev))
        def _():
            pl.semaphore_wait(barrier, 2)

        @pl.when(jnp.logical_not(has_prev))
        def _():
            got_s[:, 0:1] = jnp.full((chunks, 1, 2 * cb), -1e30, F32)
            got_s[:, 1:2] = jnp.zeros((chunks, 1, 2 * cb), F32)
            got_o[...] = jnp.zeros(got_o.shape, BF16)
            got_dq[...] = jnp.zeros(got_dq.shape, BF16)
            kv[:, :, 2 * both :, :] = jnp.zeros((chunks, 2, pb, PAIR), BF16)

        @pl.when(jnp.logical_not(has_next))
        def _():
            theirs[...] = jnp.zeros(theirs.shape, BF16)
            their_bias[...] = jnp.zeros(their_bias.shape, F32)
            got_back[...] = jnp.zeros(got_back.shape, F32)
            got_far[...] = jnp.zeros(got_far.shape, BF16)


        @pl.when(even & has_prev)
        def _():
            for c in range(QUERY_AHEAD):
                send_queries(c)

        @pl.when(odd & has_next)
        def _():
            for c in range(FAR_AHEAD):
                send_far(c)

        for c in range(SIB_AHEAD):
            send_sib(c)
        near_cont = jnp.where(
            start_ref[0] <= j - 1, valid_ref[jnp.maximum(j - 1, 0)], 0
        )
        own_len = valid_ref[j]
        limits = [jnp.where(links_ref[0, d] > 0, pb, 0) for d in range(3)]
        far_key = lax.broadcasted_iota(jnp.int32, row_bias.shape, 1)
        far_limit = jnp.where(
            far_key < pb,
            limits[2],
            jnp.where(far_key < 2 * pb, limits[1] + pb, near_cont + 2 * pb),
        )
        row_bias[...] = jnp.where(far_key < far_limit, 0.0, -1e30)

        @pl.when(even & has_prev)
        def _():
            send(row_bias, their_bias, rb_out, rb_in, prv)

        key = lax.broadcasted_iota(jnp.int32, (cb, 2 * both + pb), 1)
        query = lax.broadcasted_iota(jnp.int32, (cb, 2 * both + pb), 0)
        limit = jnp.where(
            key < cb,
            jnp.minimum(query, own_len - 1) + 1,
            jnp.where(
                key < both,
                limits[0] + cb,
                jnp.where(
                    key < both + pb,
                    limits[1] + both,
                    jnp.where(
                        key < 2 * both, near_cont + (both + pb), limits[2] + 2 * both
                    ),
                ),
            ),
        )
        bias[...] = jnp.where(key < limit, 0.0, -1e30)

        @pl.when(even & has_next)
        def _():
            wait_bytes(their_bias, rb_in)

    @pl.when((step > 0) & (step + SIB_AHEAD <= chunks))
    def _():
        send_sib(step + SIB_AHEAD - 1)

    @pl.when((step > 0) & (step + QUERY_AHEAD <= chunks) & even & has_prev)
    def _():
        send_queries(step + QUERY_AHEAD - 1)

    @pl.when((step > 0) & (step + FAR_AHEAD <= chunks) & odd & has_next)
    def _():
        send_far(step + FAR_AHEAD - 1)

    @pl.when((step < chunks) & odd)
    def _():
        c = step
        wait_bytes(own_rows(c), kv_in.at[c])
        wait_bytes(mine.at[c], q_in.at[c])
        wait_bytes(sib_rows(c), sib_in.at[c])

        @pl.when(has_prev)
        def _():
            wait_bytes(far_rows(c), far_in.at[c])

        live, qs, gs = rows_of(mine, c, j)
        k = kv[c, 0]
        v = kv[c, 1]
        b = bias[...]
        s = mm_t(qs, k) + jnp.concatenate([b, b], 0)
        top, total, e, out = softmax_parts(s, v)
        inverse = jnp.broadcast_to(1.0 / total, out.shape)
        out = out * inverse
        put_o(c, jnp.where(live, folded(out), 0.0))
        delta = jnp.broadcast_to(row_dot(gs, out), out.shape)
        dq, grads = gradients(e, qs, gs, k, v, delta, inverse)
        put_dq(c, dq)
        for which in range(2):
            own[lax.rem(c, slots), which] = grads[which][:both]
            sib_g[c, which] = grads[which][both : 2 * both].astype(BF16)
            far_g[c, which] = grads[which][2 * both :].astype(BF16)

        @pl.when(has_prev)
        def _():
            send(far_g.at[c], got_far.at[c], fg_out.at[c], fg_in.at[c], prv)

        send(sib_g.at[c], got_sib.at[c], sg_out.at[c], sg_in.at[c], sib)

    def wait_first(c):
        wait_bytes(own_rows(c), kv_in.at[c])
        wait_bytes(mine.at[c], q_in.at[c])
        wait_bytes(sib_rows(c), sib_in.at[c])

        @pl.when(has_next)
        def _():
            wait_bytes(theirs.at[c], qg_in.at[c])

    def wait_merge(c):
        @pl.when(has_prev)
        def _():
            wait_bytes(got_s.at[c], s_in.at[c])
            wait_bytes(got_o.at[c], o_in.at[c])

    def wait_back(c):
        @pl.when(has_next)
        def _():
            wait_bytes(got_back.at[c], b_in.at[c])

    def first(c):
        slot = lax.rem(c, e_slots)
        _, qs, gs = rows_of(theirs, c, nxt)
        k = kv[c, 0, cb : 2 * both]
        v = kv[c, 1, cb : 2 * both]
        s = mm_t(qs, k) + their_bias[0:1, :]
        top, total, e, out = softmax_parts(s, v)
        part_o[c] = folded(out * (1.0 / total)).astype(BF16)
        top, total, delta = as_rows(top, total, row_dot(gs, out))
        part_s[c, 0:1] = (top + jnp.log(total)) * LOG2E
        part_s[c, 1:2] = delta / total
        exps[slot] = e
        sums[slot, 0:1] = total

    def merge(c):
        slot = lax.rem(c, slots)
        live, qs, gs = rows_of(mine, c, j)
        k = kv[c, 0, :both]
        v = kv[c, 1, :both]
        b = bias[:, :both]
        s = mm_t(qs, k) + jnp.concatenate([b, b], 0)
        top, total, e, out = softmax_parts(s, v)
        top, total, delta = as_rows(top, total, row_dot(gs, out))
        level = (top + jnp.log(total)) * LOG2E
        far_level = got_s[c, 0:1]
        high = jnp.maximum(level, far_level)
        mix = high + jnp.log(jnp.exp2(level - high) + jnp.exp2(far_level - high)) * LOG2E
        factor = jnp.exp2(level - mix) / total
        far_share = jnp.exp2(far_level - mix)
        delta = factor * delta + far_share * got_s[c, 1:2]
        back_s[c, 0:1] = far_share
        back_s[c, 1:2] = delta
        factor = spread(factor)
        mixed = folded(out * factor) + folded(spread(far_share)) * got_o[c].astype(F32)
        out_o[c] = jnp.where(live, mixed, 0.0).astype(BF16)
        dq, grads = gradients(e, qs, gs, k, v, spread(delta), factor)
        own_dq[slot] = dq
        for which in range(2):
            own[slot, which] = grads[which]

    def back(c):
        slot = lax.rem(c, e_slots)
        _, qs, gs = rows_of(theirs, c, nxt)
        k = kv[c, 0, cb : 2 * both]
        v = kv[c, 1, cb : 2 * both]
        factor = spread(got_back[c, 0:1] / sums[slot, 0:1])
        delta = spread(got_back[c, 1:2])
        dq, grads = gradients(exps[slot], qs, gs, k, v, delta, factor)
        part_dq[c] = dq.astype(BF16)
        for which in range(2):
            own[lax.rem(c, slots), which, cb:, :] += grads[which][:pb]
            sib_g[c, which] = grads[which][pb:].astype(BF16)

    def send_first(c):
        @pl.when(has_next)
        def _():
            send(part_s.at[c], got_s.at[c], s_out.at[c], s_in.at[c], nxt)
            send(part_o.at[c], got_o.at[c], o_out.at[c], o_in.at[c], nxt)

    def send_merge(c):
        @pl.when(has_prev)
        def _():
            send(back_s.at[c], got_back.at[c], b_out.at[c], b_in.at[c], prv)

        pltpu.make_async_copy(out_o.at[c], o_ref.at[:, cols(c)], res_o.at[c]).start()

    def send_back(c):
        @pl.when(has_next)
        def _():
            send(part_dq.at[c], got_dq.at[c], dq_out.at[c], dq_in.at[c], nxt)

        send(sib_g.at[c], got_sib.at[c], sg_out.at[c], sg_in.at[c], sib)

    at_merge = step - MERGE_LAG
    at_back = step - BACK_LAG
    steady = (at_back >= 0) & (step < chunks)

    @pl.when(steady & even)
    def _():
        wait_back(at_back)
        wait_merge(at_merge)
        wait_first(step)
        merge(at_merge)
        back(at_back)
        first(step)
        send_merge(at_merge)
        send_first(step)
        send_back(at_back)

    @pl.when((step < BACK_LAG) & even)
    def _():
        wait_first(step)
        first(step)
        send_first(step)

    @pl.when((at_merge >= 0) & (at_merge < chunks) & even & jnp.logical_not(steady))
    def _():
        wait_merge(at_merge)
        merge(at_merge)
        send_merge(at_merge)

    @pl.when((step >= chunks) & (at_back < chunks) & even)
    def _():
        wait_back(at_back)
        back(at_back)
        send_back(at_back)

    @pl.when(step >= LAG)
    def _():
        c = step - LAG
        slot = lax.rem(c, slots)

        @pl.when(odd)
        def _():
            @pl.when(has_next)
            def _():
                wait_bytes(got_far.at[c], fg_in.at[c])

            own[slot, :, cb:, :] += got_far[c].astype(F32)

        @pl.when(even)
        def _():
            @pl.when(has_prev)
            def _():
                wait_bytes(got_dq.at[c], dq_in.at[c])

            put_dq(c, own_dq[slot] + got_dq[c].astype(F32))

        wait_bytes(got_sib.at[c], sg_in.at[c])
        for which, (cont, prompt) in enumerate(((ckg_ref, pkg_ref), (cvg_ref, pvg_ref))):
            out_g[c, which, :cb, :] = (
                own[slot, which, :cb, :] + got_sib[c, which, pb:, :].astype(F32)
            ).astype(BF16)
            out_g[c, which, cb:, :] = (
                own[slot, which, cb:, :] + got_sib[c, which, :pb, :].astype(F32)
            ).astype(BF16)
            pltpu.make_async_copy(
                out_g.at[c, which, pl.ds(0, cb)], cont.at[:, cols(c)], res_g.at[c]
            ).start()
            pltpu.make_async_copy(
                out_g.at[c, which, pl.ds(cb, pb)], prompt.at[:, cols(c)], res_g.at[c]
            ).start()

    @pl.when(step == chunks + LAG - 1)
    def _():
        def finish(c, carry):
            wait_bytes(sib_rows(c), sib_out.at[c])
            wait_bytes(sib_g.at[c], sg_out.at[c])
            wait_bytes(out_o.at[c], res_o.at[c])
            wait_bytes(out_dq.at[c], res_dq.at[c])
            wait_bytes(out_g.at[c], res_g.at[c])

            @pl.when(even & has_prev)
            def _():
                wait_bytes(theirs.at[c], qg_out.at[c])
                wait_bytes(back_s.at[c], b_out.at[c])

            @pl.when(even & has_next)
            def _():
                wait_bytes(part_o.at[c], o_out.at[c])
                wait_bytes(part_s.at[c], s_out.at[c])
                wait_bytes(part_dq.at[c], dq_out.at[c])

            @pl.when(odd & has_next)
            def _():
                wait_bytes(far_rows(c), far_out.at[c])

            @pl.when(odd & has_prev)
            def _():
                wait_bytes(far_g.at[c], fg_out.at[c])

            return carry

        lax.fori_loop(0, chunks, finish, 0)

        @pl.when(even & has_prev)
        def _():
            wait_bytes(row_bias, rb_out)


def hand_over(*refs):
    count = (len(refs) - 2) // 3
    sources, targets, held = refs[:count], refs[count : 2 * count], refs[2 * count : 3 * count]
    sems_in, sems_out = refs[-2:]
    loads = [
        pltpu.make_async_copy(sources[i], held[i], sems_in.at[i]) for i in range(count)
    ]
    stores = [
        pltpu.make_async_copy(held[i], targets[i], sems_out.at[i]) for i in range(count)
    ]
    for load in loads:
        load.start()
    for load, store in zip(loads, stores):
        load.wait()
        store.start()
    for store in stores:
        store.wait()


def per_device(*args):
    q, ck, cv, pk, pv, g, links, start, valid = args
    cb, width = q.shape
    pb = pk.shape[0]
    chunks = width // PAIR
    length = lax.axis_size("ctx")
    keys = 2 * cb + 3 * pb
    both = cb + pb
    far_keys = cb + 2 * pb
    anywhere = pl.BlockSpec(memory_space=pl.ANY)
    scalars = pl.BlockSpec(memory_space=pltpu.SMEM)
    wide = jax.ShapeDtypeStruct((cb, width), BF16)
    short = jax.ShapeDtypeStruct((pb, width), BF16)
    work = 12 * cb * keys * width
    rows = pltpu.VMEM((chunks, cb, PAIR), BF16)
    stats = pltpu.VMEM((chunks, 2, 2 * cb), F32)
    pair_rows = pltpu.VMEM((chunks, 2, cb, PAIR), BF16)
    sib_grad = pltpu.VMEM((chunks, 2, both, PAIR), BF16)
    far_grad = pltpu.VMEM((chunks, 2, pb, PAIR), BF16)
    results = pl.pallas_call(
        functools.partial(kernel, chunks, length),
        grid=(chunks + LAG,),
        in_specs=[anywhere] * 6 + [scalars] * 3,
        out_specs=[anywhere] * 6,
        out_shape=[wide, wide, wide, wide, short, short],
        scratch_shapes=[
            pltpu.VMEM((chunks, 2, keys, PAIR), BF16),
            pair_rows,
            pair_rows,
            pltpu.VMEM((cb, keys), F32),
            pltpu.VMEM((8, far_keys), F32),
            pltpu.VMEM((8, far_keys), F32),
            pltpu.VMEM((BACK_LAG + 1, 2 * cb, far_keys), BF16),
            pltpu.VMEM((BACK_LAG + 1, 2, 2 * cb), F32),
            pltpu.VMEM((LAG + 1, 2, both, PAIR), F32),
            pltpu.VMEM((LAG + 1, cb, PAIR), F32),
            rows,
            rows,
            stats,
            stats,
            stats,
            stats,
            rows,
            rows,
            sib_grad,
            sib_grad,
            far_grad,
            far_grad,
            rows,
            rows,
            sib_grad,
        ]
        + [pltpu.SemaphoreType.DMA((chunks,))] * 23
        + [pltpu.SemaphoreType.DMA] * 2,
        compiler_params=pltpu.CompilerParams(
            collective_id=0, has_side_effects=True, vmem_limit_bytes=60 * 2**20
        ),
        cost_estimate=pl.CostEstimate(
            flops=work, bytes_accessed=12 * 2 * cb * width, transcendentals=cb * keys * width // HD
        ),
        name="pairs",
    )(q, g, ck, cv, pk, pv, links, start, valid)
    return pl.pallas_call(
        hand_over,
        in_specs=[anywhere] * 6,
        out_specs=[anywhere] * 6,
        out_shape=[wide, wide, wide, wide, short, short],
        scratch_shapes=[pltpu.VMEM(shape.shape, BF16) for shape in (wide,) * 4 + (short,) * 2]
        + [pltpu.SemaphoreType.DMA((6,))] * 2,
        name="hand_over",
    )(*results)


def solution(mesh):
    rows = P(("dp", "ctx"), None)
    return jax.shard_map(
        per_device,
        mesh=mesh,
        in_specs=(rows,) * 7 + (P(("dp", "ctx")), P("dp")),
        out_specs=(rows,) * 6,
        check_vma=False,
    )
```

```python
import functools

import jax
import jax.numpy as jnp
from jax import lax
from jax.experimental import pallas as pl
from jax.experimental.pallas import tpu as pltpu
from jax.sharding import PartitionSpec as P

HD = 64
PAIR = 2 * HD
QUERY_AHEAD = 3
FAR_AHEAD = 4
SIB_AHEAD = 3
MERGE_LAG = 2
RETURN_LAG = 4
BACK_LAG = 4
LAG = 7
SCALE = HD ** (-0.5)
LOG2E = 1.4426950408889634
F32 = jnp.float32
BF16 = jnp.bfloat16
MESH = pl.DeviceIdType.MESH


def mm(a, b):
    return lax.dot_general(a, b, (((1,), (0,)), ((), ())), preferred_element_type=F32)


def mm_t(a, b):
    return lax.dot_general(a, b, (((1,), (1,)), ((), ())), preferred_element_type=F32)


def stacked(x):
    first = lax.broadcasted_iota(jnp.int32, x.shape, 1) < HD
    zero = jnp.zeros((), x.dtype)
    return jnp.concatenate([jnp.where(first, x, zero), jnp.where(first, zero, x)], 0)


def folded(x):
    half = x.shape[0] // 2
    first = lax.broadcasted_iota(jnp.int32, (half, PAIR), 1) < HD
    return jnp.where(first, x[:half], x[half:])


def as_rows(a, b, c):
    lane = lax.broadcasted_iota(jnp.int32, (a.shape[0], PAIR), 1)
    turned = jnp.where(lane == 0, a, jnp.where(lane == 1, b, c)).T
    return turned[0:1], turned[1:2], turned[2:3]


def spread(row):
    return jnp.broadcast_to(row, (PAIR, row.shape[1])).T


def repeated(x, count):
    return jnp.concatenate([x] * (-(-count // PAIR)), 1)[:, :count]


def softmax_parts(s, v):
    top = jnp.max(s, axis=1, keepdims=True)
    e = jnp.exp2((s - top) * LOG2E)
    total = jnp.sum(e, axis=1, keepdims=True)
    e = e.astype(BF16)
    return top, total, e, mm(e, v)


def row_dot(gs, out):
    return jnp.sum(gs.astype(F32) * out, axis=1, keepdims=True)


def gradients(e, qs, gs, k, v, delta, factor):
    shifted = mm_t(gs, v) - repeated(delta, k.shape[0])
    ds = (e.astype(F32) * shifted).astype(BF16)
    dq = folded(mm(ds, k) * (factor * SCALE))
    dk = mm((qs.astype(F32) * factor).astype(BF16).T, ds).T
    dv = mm((gs.astype(F32) * factor).astype(BF16).T, e).T
    return dq, (dk, dv)


def kernel(
    chunks,
    length,
    q_ref,
    g_ref,
    ck_ref,
    cv_ref,
    pk_ref,
    pv_ref,
    links_ref,
    start_ref,
    valid_ref,
    o_ref,
    dq_ref,
    ckg_ref,
    cvg_ref,
    pkg_ref,
    pvg_ref,
    kv,
    mine,
    theirs,
    bias,
    row_bias,
    their_bias,
    exps,
    sums,
    own,
    own_dq,
    part_o,
    got_o,
    part_s,
    got_s,
    back_s,
    got_back,
    part_dq,
    got_dq,
    sib_g,
    got_sib,
    far_g,
    got_far,
    out_o,
    out_dq,
    out_g,
    kv_in,
    q_in,
    sib_out,
    sib_in,
    far_out,
    far_in,
    qg_out,
    qg_in,
    o_out,
    o_in,
    s_out,
    s_in,
    b_out,
    b_in,
    dq_out,
    dq_in,
    sg_out,
    sg_in,
    fg_out,
    fg_in,
    res_o,
    res_dq,
    res_g,
    rb_out,
    rb_in,
):
    step = pl.program_id(0)
    cb = ck_ref.shape[0]
    pb = pk_ref.shape[0]
    both = cb + pb
    j = lax.axis_index("ctx")
    parity = lax.rem(j, 2)
    even = parity == 0
    odd = parity == 1
    sib = j + 1 - 2 * parity
    nxt = lax.rem(j + 2, length)
    prv = lax.rem(j + length - 2, length)
    has_next = j + 2 < length
    has_prev = j >= 2
    slots = own.shape[0]
    e_slots = exps.shape[0]

    def cols(c):
        return pl.ds(pl.multiple_of(c * PAIR, PAIR), PAIR)

    def send(src, dst, out_sem, in_sem, to):
        pltpu.make_async_remote_copy(
            src_ref=src,
            dst_ref=dst,
            send_sem=out_sem,
            recv_sem=in_sem,
            device_id={"ctx": to},
            device_id_type=MESH,
        ).start()

    def wait_bytes(ref, sem):
        pltpu.make_async_copy(ref, ref, sem).wait()

    def own_rows(c):
        return kv.at[c, :, pl.ds(0, both)]

    def sib_rows(c):
        return kv.at[c, :, pl.ds(both, both)]

    def far_rows(c):
        return kv.at[c, :, pl.ds(2 * both, pb)]

    def send_far(c):
        for which, prompt in enumerate((pk_ref, pv_ref)):
            send(
                prompt.at[:, cols(c)],
                kv.at[c, which, pl.ds(2 * both, pb)],
                far_out.at[c],
                far_in.at[c],
                nxt,
            )

    def send_queries(c):
        send(q_ref.at[:, cols(c)], theirs.at[c, 0], qg_out.at[c], qg_in.at[c], prv)
        send(g_ref.at[:, cols(c)], theirs.at[c, 1], qg_out.at[c], qg_in.at[c], prv)

    def send_sib(c):
        for which, (cont, prompt) in enumerate(((ck_ref, pk_ref), (cv_ref, pv_ref))):
            cont_c, prompt_c = cont.at[:, cols(c)], prompt.at[:, cols(c)]
            send(
                prompt_c, kv.at[c, which, pl.ds(both, pb)], sib_out.at[c], sib_in.at[c], sib
            )
            send(
                cont_c,
                kv.at[c, which, pl.ds(both + pb, cb)],
                sib_out.at[c],
                sib_in.at[c],
                sib,
            )
            pltpu.make_async_copy(cont_c, kv.at[c, which, pl.ds(0, cb)], kv_in.at[c]).start()
            pltpu.make_async_copy(prompt_c, kv.at[c, which, pl.ds(cb, pb)], kv_in.at[c]).start()
        pltpu.make_async_copy(q_ref.at[:, cols(c)], mine.at[c, 0], q_in.at[c]).start()
        pltpu.make_async_copy(g_ref.at[:, cols(c)], mine.at[c, 1], q_in.at[c]).start()

    def rows_of(ref, c, block):
        live = lax.broadcasted_iota(jnp.int32, (cb, 1), 0) < valid_ref[block]
        qs = stacked(ref[c, 0] * jnp.asarray(SCALE, BF16))
        gs = stacked(jnp.where(live, ref[c, 1].astype(F32), 0.0)).astype(BF16)
        return live, qs, gs

    def put_o(c, value):
        out_o[c] = value.astype(BF16)
        pltpu.make_async_copy(out_o.at[c], o_ref.at[:, cols(c)], res_o.at[c]).start()

    def put_dq(c, value):
        out_dq[c] = value.astype(BF16)
        pltpu.make_async_copy(out_dq.at[c], dq_ref.at[:, cols(c)], res_dq.at[c]).start()

    @pl.when(step == 0)
    def _():
        barrier = pltpu.get_barrier_semaphore()

        def greet(other):
            pl.semaphore_signal(barrier, inc=1, device_id={"ctx": other}, device_id_type=MESH)

        greet(sib)

        @pl.when(has_next)
        def _():
            greet(nxt)

        @pl.when(has_prev)
        def _():
            greet(prv)

        @pl.when(has_next & has_prev)
        def _():
            pl.semaphore_wait(barrier, 3)

        @pl.when(jnp.logical_not(has_next & has_prev))
        def _():
            pl.semaphore_wait(barrier, 2)

        @pl.when(jnp.logical_not(has_prev))
        def _():
            got_s[:, 0:1] = jnp.full((chunks, 1, 2 * cb), -1e30, F32)
            got_s[:, 1:2] = jnp.zeros((chunks, 1, 2 * cb), F32)
            got_o[...] = jnp.zeros(got_o.shape, BF16)
            got_dq[...] = jnp.zeros(got_dq.shape, BF16)
            kv[:, :, 2 * both :, :] = jnp.zeros((chunks, 2, pb, PAIR), BF16)

        @pl.when(jnp.logical_not(has_next))
        def _():
            theirs[...] = jnp.zeros(theirs.shape, BF16)
            their_bias[...] = jnp.zeros(their_bias.shape, F32)
            got_back[...] = jnp.zeros(got_back.shape, F32)
            got_far[...] = jnp.zeros(got_far.shape, BF16)


        @pl.when(even & has_prev)
        def _():
            for c in range(QUERY_AHEAD):
                send_queries(c)

        @pl.when(odd & has_next)
        def _():
            for c in range(FAR_AHEAD):
                send_far(c)

        for c in range(SIB_AHEAD):
            send_sib(c)
        near_cont = jnp.where(
            start_ref[0] <= j - 1, valid_ref[jnp.maximum(j - 1, 0)], 0
        )
        own_len = valid_ref[j]
        limits = [jnp.where(links_ref[0, d] > 0, pb, 0) for d in range(3)]
        far_key = lax.broadcasted_iota(jnp.int32, row_bias.shape, 1)
        far_limit = jnp.where(
            far_key < pb,
            limits[2],
            jnp.where(far_key < 2 * pb, limits[1] + pb, near_cont + 2 * pb),
        )
        row_bias[...] = jnp.where(far_key < far_limit, 0.0, -1e30)

        @pl.when(even & has_prev)
        def _():
            send(row_bias, their_bias, rb_out, rb_in, prv)

        key = lax.broadcasted_iota(jnp.int32, (cb, 2 * both + pb), 1)
        query = lax.broadcasted_iota(jnp.int32, (cb, 2 * both + pb), 0)
        limit = jnp.where(
            key < cb,
            jnp.minimum(query, own_len - 1) + 1,
            jnp.where(
                key < both,
                limits[0] + cb,
                jnp.where(
                    key < both + pb,
                    limits[1] + both,
                    jnp.where(
                        key < 2 * both, near_cont + (both + pb), limits[2] + 2 * both
                    ),
                ),
            ),
        )
        bias[...] = jnp.where(key < limit, 0.0, -1e30)

        @pl.when(even & has_next)
        def _():
            wait_bytes(their_bias, rb_in)

    @pl.when((step > 0) & (step + SIB_AHEAD <= chunks))
    def _():
        send_sib(step + SIB_AHEAD - 1)

    @pl.when((step > 0) & (step + QUERY_AHEAD <= chunks) & even & has_prev)
    def _():
        send_queries(step + QUERY_AHEAD - 1)

    @pl.when((step > 0) & (step + FAR_AHEAD <= chunks) & odd & has_next)
    def _():
        send_far(step + FAR_AHEAD - 1)

    @pl.when((step >= RETURN_LAG) & (step < chunks + RETURN_LAG) & odd & has_prev)
    def _():
        c = step - RETURN_LAG
        send(far_g.at[c], got_far.at[c], fg_out.at[c], fg_in.at[c], prv)

    @pl.when((step < chunks) & odd)
    def _():
        c = step
        wait_bytes(own_rows(c), kv_in.at[c])
        wait_bytes(mine.at[c], q_in.at[c])
        wait_bytes(sib_rows(c), sib_in.at[c])

        @pl.when(has_prev)
        def _():
            wait_bytes(far_rows(c), far_in.at[c])

        live, qs, gs = rows_of(mine, c, j)
        k = kv[c, 0]
        v = kv[c, 1]
        b = bias[...]
        s = mm_t(qs, k) + jnp.concatenate([b, b], 0)
        top, total, e, out = softmax_parts(s, v)
        inverse = jnp.broadcast_to(1.0 / total, out.shape)
        out = out * inverse
        put_o(c, jnp.where(live, folded(out), 0.0))
        delta = jnp.broadcast_to(row_dot(gs, out), out.shape)
        dq, grads = gradients(e, qs, gs, k, v, delta, inverse)
        put_dq(c, dq)
        for which in range(2):
            own[lax.rem(c, slots), which] = grads[which][:both]
            sib_g[c, which] = grads[which][both : 2 * both].astype(BF16)
            far_g[c, which] = grads[which][2 * both :].astype(BF16)
        send(sib_g.at[c], got_sib.at[c], sg_out.at[c], sg_in.at[c], sib)

    def wait_first(c):
        wait_bytes(own_rows(c), kv_in.at[c])
        wait_bytes(mine.at[c], q_in.at[c])
        wait_bytes(sib_rows(c), sib_in.at[c])

        @pl.when(has_next)
        def _():
            wait_bytes(theirs.at[c], qg_in.at[c])

    def wait_merge(c):
        @pl.when(has_prev)
        def _():
            wait_bytes(got_s.at[c], s_in.at[c])
            wait_bytes(got_o.at[c], o_in.at[c])

    def wait_back(c):
        @pl.when(has_next)
        def _():
            wait_bytes(got_back.at[c], b_in.at[c])

    def first(c):
        slot = lax.rem(c, e_slots)
        _, qs, gs = rows_of(theirs, c, nxt)
        k = kv[c, 0, cb : 2 * both]
        v = kv[c, 1, cb : 2 * both]
        s = mm_t(qs, k) + their_bias[0:1, :]
        top, total, e, out = softmax_parts(s, v)
        part_o[c] = folded(out * (1.0 / total)).astype(BF16)
        top, total, delta = as_rows(top, total, row_dot(gs, out))
        part_s[c, 0:1] = (top + jnp.log(total)) * LOG2E
        part_s[c, 1:2] = delta / total
        exps[slot] = e
        sums[slot, 0:1] = total

    def merge(c):
        slot = lax.rem(c, slots)
        live, qs, gs = rows_of(mine, c, j)
        k = kv[c, 0, :both]
        v = kv[c, 1, :both]
        b = bias[:, :both]
        s = mm_t(qs, k) + jnp.concatenate([b, b], 0)
        top, total, e, out = softmax_parts(s, v)
        top, total, delta = as_rows(top, total, row_dot(gs, out))
        level = (top + jnp.log(total)) * LOG2E
        far_level = got_s[c, 0:1]
        high = jnp.maximum(level, far_level)
        mix = high + jnp.log(jnp.exp2(level - high) + jnp.exp2(far_level - high)) * LOG2E
        factor = jnp.exp2(level - mix) / total
        far_share = jnp.exp2(far_level - mix)
        delta = factor * delta + far_share * got_s[c, 1:2]
        back_s[c, 0:1] = far_share
        back_s[c, 1:2] = delta
        factor = spread(factor)
        mixed = folded(out * factor) + folded(spread(far_share)) * got_o[c].astype(F32)
        out_o[c] = jnp.where(live, mixed, 0.0).astype(BF16)
        dq, grads = gradients(e, qs, gs, k, v, spread(delta), factor)
        own_dq[slot] = dq
        for which in range(2):
            own[slot, which] = grads[which]

    def back(c):
        slot = lax.rem(c, e_slots)
        _, qs, gs = rows_of(theirs, c, nxt)
        k = kv[c, 0, cb : 2 * both]
        v = kv[c, 1, cb : 2 * both]
        factor = spread(got_back[c, 0:1] / sums[slot, 0:1])
        delta = spread(got_back[c, 1:2])
        dq, grads = gradients(exps[slot], qs, gs, k, v, delta, factor)
        part_dq[c] = dq.astype(BF16)
        for which in range(2):
            own[lax.rem(c, slots), which, cb:, :] += grads[which][:pb]
            sib_g[c, which] = grads[which][pb:].astype(BF16)

    def send_first(c):
        @pl.when(has_next)
        def _():
            send(part_s.at[c], got_s.at[c], s_out.at[c], s_in.at[c], nxt)
            send(part_o.at[c], got_o.at[c], o_out.at[c], o_in.at[c], nxt)

    def send_merge(c):
        @pl.when(has_prev)
        def _():
            send(back_s.at[c], got_back.at[c], b_out.at[c], b_in.at[c], prv)

        pltpu.make_async_copy(out_o.at[c], o_ref.at[:, cols(c)], res_o.at[c]).start()

    def send_back(c):
        @pl.when(has_next)
        def _():
            send(part_dq.at[c], got_dq.at[c], dq_out.at[c], dq_in.at[c], nxt)

        send(sib_g.at[c], got_sib.at[c], sg_out.at[c], sg_in.at[c], sib)

    at_merge = step - MERGE_LAG
    at_back = step - BACK_LAG
    steady = (at_back >= 0) & (step < chunks)

    @pl.when(steady & even)
    def _():
        wait_back(at_back)
        wait_merge(at_merge)
        wait_first(step)
        merge(at_merge)
        back(at_back)
        first(step)
        send_merge(at_merge)
        send_first(step)
        send_back(at_back)

    @pl.when((step < BACK_LAG) & even)
    def _():
        wait_first(step)
        first(step)
        send_first(step)

    @pl.when((at_merge >= 0) & (at_merge < chunks) & even & jnp.logical_not(steady))
    def _():
        wait_merge(at_merge)
        merge(at_merge)
        send_merge(at_merge)

    @pl.when((step >= chunks) & (at_back < chunks) & even)
    def _():
        wait_back(at_back)
        back(at_back)
        send_back(at_back)

    @pl.when(step >= LAG)
    def _():
        c = step - LAG
        slot = lax.rem(c, slots)

        @pl.when(odd)
        def _():
            @pl.when(has_next)
            def _():
                wait_bytes(got_far.at[c], fg_in.at[c])

            own[slot, :, cb:, :] += got_far[c].astype(F32)

        @pl.when(even)
        def _():
            @pl.when(has_prev)
            def _():
                wait_bytes(got_dq.at[c], dq_in.at[c])

            put_dq(c, own_dq[slot] + got_dq[c].astype(F32))

        wait_bytes(got_sib.at[c], sg_in.at[c])
        for which, (cont, prompt) in enumerate(((ckg_ref, pkg_ref), (cvg_ref, pvg_ref))):
            out_g[c, which, :cb, :] = (
                own[slot, which, :cb, :] + got_sib[c, which, pb:, :].astype(F32)
            ).astype(BF16)
            out_g[c, which, cb:, :] = (
                own[slot, which, cb:, :] + got_sib[c, which, :pb, :].astype(F32)
            ).astype(BF16)
            pltpu.make_async_copy(
                out_g.at[c, which, pl.ds(0, cb)], cont.at[:, cols(c)], res_g.at[c]
            ).start()
            pltpu.make_async_copy(
                out_g.at[c, which, pl.ds(cb, pb)], prompt.at[:, cols(c)], res_g.at[c]
            ).start()

    @pl.when(step == chunks + LAG - 1)
    def _():
        def finish(c, carry):
            wait_bytes(sib_rows(c), sib_out.at[c])
            wait_bytes(sib_g.at[c], sg_out.at[c])
            wait_bytes(out_o.at[c], res_o.at[c])
            wait_bytes(out_dq.at[c], res_dq.at[c])
            wait_bytes(out_g.at[c], res_g.at[c])

            @pl.when(even & has_prev)
            def _():
                wait_bytes(theirs.at[c], qg_out.at[c])
                wait_bytes(back_s.at[c], b_out.at[c])

            @pl.when(even & has_next)
            def _():
                wait_bytes(part_o.at[c], o_out.at[c])
                wait_bytes(part_s.at[c], s_out.at[c])
                wait_bytes(part_dq.at[c], dq_out.at[c])

            @pl.when(odd & has_next)
            def _():
                wait_bytes(far_rows(c), far_out.at[c])

            @pl.when(odd & has_prev)
            def _():
                wait_bytes(far_g.at[c], fg_out.at[c])

            return carry

        lax.fori_loop(0, chunks, finish, 0)

        @pl.when(even & has_prev)
        def _():
            wait_bytes(row_bias, rb_out)


def hand_over(*refs):
    count = (len(refs) - 2) // 3
    sources, targets, held = refs[:count], refs[count : 2 * count], refs[2 * count : 3 * count]
    sems_in, sems_out = refs[-2:]
    loads = [
        pltpu.make_async_copy(sources[i], held[i], sems_in.at[i]) for i in range(count)
    ]
    stores = [
        pltpu.make_async_copy(held[i], targets[i], sems_out.at[i]) for i in range(count)
    ]
    for load in loads:
        load.start()
    for load, store in zip(loads, stores):
        load.wait()
        store.start()
    for store in stores:
        store.wait()


def per_device(*args):
    q, ck, cv, pk, pv, g, links, start, valid = args
    cb, width = q.shape
    pb = pk.shape[0]
    chunks = width // PAIR
    length = lax.axis_size("ctx")
    keys = 2 * cb + 3 * pb
    both = cb + pb
    far_keys = cb + 2 * pb
    anywhere = pl.BlockSpec(memory_space=pl.ANY)
    scalars = pl.BlockSpec(memory_space=pltpu.SMEM)
    wide = jax.ShapeDtypeStruct((cb, width), BF16)
    short = jax.ShapeDtypeStruct((pb, width), BF16)
    work = 12 * cb * keys * width
    rows = pltpu.VMEM((chunks, cb, PAIR), BF16)
    stats = pltpu.VMEM((chunks, 2, 2 * cb), F32)
    pair_rows = pltpu.VMEM((chunks, 2, cb, PAIR), BF16)
    sib_grad = pltpu.VMEM((chunks, 2, both, PAIR), BF16)
    far_grad = pltpu.VMEM((chunks, 2, pb, PAIR), BF16)
    results = pl.pallas_call(
        functools.partial(kernel, chunks, length),
        grid=(chunks + LAG,),
        in_specs=[anywhere] * 6 + [scalars] * 3,
        out_specs=[anywhere] * 6,
        out_shape=[wide, wide, wide, wide, short, short],
        scratch_shapes=[
            pltpu.VMEM((chunks, 2, keys, PAIR), BF16),
            pair_rows,
            pair_rows,
            pltpu.VMEM((cb, keys), F32),
            pltpu.VMEM((8, far_keys), F32),
            pltpu.VMEM((8, far_keys), F32),
            pltpu.VMEM((BACK_LAG + 1, 2 * cb, far_keys), BF16),
            pltpu.VMEM((BACK_LAG + 1, 2, 2 * cb), F32),
            pltpu.VMEM((LAG + 1, 2, both, PAIR), F32),
            pltpu.VMEM((LAG + 1, cb, PAIR), F32),
            rows,
            rows,
            stats,
            stats,
            stats,
            stats,
            rows,
            rows,
            sib_grad,
            sib_grad,
            far_grad,
            far_grad,
            rows,
            rows,
            sib_grad,
        ]
        + [pltpu.SemaphoreType.DMA((chunks,))] * 23
        + [pltpu.SemaphoreType.DMA] * 2,
        compiler_params=pltpu.CompilerParams(
            collective_id=0, has_side_effects=True, vmem_limit_bytes=60 * 2**20
        ),
        cost_estimate=pl.CostEstimate(
            flops=work, bytes_accessed=12 * 2 * cb * width, transcendentals=cb * keys * width // HD
        ),
        name="pairs",
    )(q, g, ck, cv, pk, pv, links, start, valid)
    return pl.pallas_call(
        hand_over,
        in_specs=[anywhere] * 6,
        out_specs=[anywhere] * 6,
        out_shape=[wide, wide, wide, wide, short, short],
        scratch_shapes=[pltpu.VMEM(shape.shape, BF16) for shape in (wide,) * 4 + (short,) * 2]
        + [pltpu.SemaphoreType.DMA((6,))] * 2,
        name="hand_over",
    )(*results)


def solution(mesh):
    rows = P(("dp", "ctx"), None)
    return jax.shard_map(
        per_device,
        mesh=mesh,
        in_specs=(rows,) * 7 + (P(("dp", "ctx")), P("dp")),
        out_specs=(rows,) * 6,
        check_vma=False,
    )
```

```python
import functools

import jax
import jax.numpy as jnp
from jax import lax
from jax.experimental import pallas as pl
from jax.experimental.pallas import tpu as pltpu
from jax.sharding import PartitionSpec as P

HD = 64
PAIR = 2 * HD
QUERY_AHEAD = 3
FAR_AHEAD = 4
SIB_AHEAD = 3
MERGE_LAG = 2
RETURN_LAG = 4
BACK_LAG = 4
LAG = 7
SCALE = HD ** (-0.5)
LOG2E = 1.4426950408889634
F32 = jnp.float32
BF16 = jnp.bfloat16
MESH = pl.DeviceIdType.MESH


def mm(a, b):
    return lax.dot_general(a, b, (((1,), (0,)), ((), ())), preferred_element_type=F32)


def mm_t(a, b):
    return lax.dot_general(a, b, (((1,), (1,)), ((), ())), preferred_element_type=F32)


def stacked(x):
    first = lax.broadcasted_iota(jnp.int32, x.shape, 1) < HD
    zero = jnp.zeros((), x.dtype)
    return jnp.concatenate([jnp.where(first, x, zero), jnp.where(first, zero, x)], 0)


def folded(x):
    half = x.shape[0] // 2
    first = lax.broadcasted_iota(jnp.int32, (half, PAIR), 1) < HD
    return jnp.where(first, x[:half], x[half:])


def as_rows(a, b, c):
    lane = lax.broadcasted_iota(jnp.int32, (a.shape[0], PAIR), 1)
    turned = jnp.where(lane == 0, a, jnp.where(lane == 1, b, c)).T
    return turned[0:1], turned[1:2], turned[2:3]


def spread(row):
    return jnp.broadcast_to(row, (PAIR, row.shape[1])).T


def repeated(x, count):
    return jnp.concatenate([x] * (-(-count // PAIR)), 1)[:, :count]


def softmax_parts(s, v):
    top = jnp.max(s, axis=1, keepdims=True)
    e = jnp.exp2((s - top) * LOG2E)
    total = jnp.sum(e, axis=1, keepdims=True)
    e = e.astype(BF16)
    return top, total, e, mm(e, v)


def row_dot(gs, out):
    return jnp.sum(gs.astype(F32) * out, axis=1, keepdims=True)


def gradients(e, qs, gs, k, v, delta, factor):
    shifted = mm_t(gs, v) - repeated(delta, k.shape[0])
    ds = (e.astype(F32) * shifted).astype(BF16)
    dq = folded(mm(ds, k) * (factor * SCALE))
    dk = mm((qs.astype(F32) * factor).astype(BF16).T, ds).T
    dv = mm((gs.astype(F32) * factor).astype(BF16).T, e).T
    return dq, (dk, dv)


def kernel(
    chunks,
    length,
    q_ref,
    g_ref,
    ck_ref,
    cv_ref,
    pk_ref,
    pv_ref,
    links_ref,
    start_ref,
    valid_ref,
    o_ref,
    dq_ref,
    ckg_ref,
    cvg_ref,
    pkg_ref,
    pvg_ref,
    kv,
    mine,
    theirs,
    bias,
    row_bias,
    their_bias,
    exps,
    sums,
    own,
    own_dq,
    part_o,
    got_o,
    part_s,
    got_s,
    back_s,
    got_back,
    part_dq,
    got_dq,
    sib_g,
    got_sib,
    far_g,
    got_far,
    out_o,
    out_dq,
    out_g,
    kv_in,
    q_in,
    sib_out,
    sib_in,
    far_out,
    far_in,
    qg_out,
    qg_in,
    o_out,
    o_in,
    s_out,
    s_in,
    b_out,
    b_in,
    dq_out,
    dq_in,
    sg_out,
    sg_in,
    fg_out,
    fg_in,
    res_o,
    res_dq,
    res_g,
    rb_out,
    rb_in,
):
    step = pl.program_id(0)
    cb = ck_ref.shape[0]
    pb = pk_ref.shape[0]
    both = cb + pb
    j = lax.axis_index("ctx")
    parity = lax.rem(j, 2)
    even = parity == 0
    odd = parity == 1
    sib = j + 1 - 2 * parity
    nxt = lax.rem(j + 2, length)
    prv = lax.rem(j + length - 2, length)
    has_next = j + 2 < length
    has_prev = j >= 2
    slots = own.shape[0]
    e_slots = exps.shape[0]

    def cols(c):
        return pl.ds(pl.multiple_of(c * PAIR, PAIR), PAIR)

    def send(src, dst, out_sem, in_sem, to):
        pltpu.make_async_remote_copy(
            src_ref=src,
            dst_ref=dst,
            send_sem=out_sem,
            recv_sem=in_sem,
            device_id={"ctx": to},
            device_id_type=MESH,
        ).start()

    def wait_bytes(ref, sem):
        pltpu.make_async_copy(ref, ref, sem).wait()

    def own_rows(c):
        return kv.at[c, :, pl.ds(0, both)]

    def sib_rows(c):
        return kv.at[c, :, pl.ds(both, both)]

    def far_rows(c):
        return kv.at[c, :, pl.ds(2 * both, pb)]

    def send_far(c):
        for which, prompt in enumerate((pk_ref, pv_ref)):
            send(
                prompt.at[:, cols(c)],
                kv.at[c, which, pl.ds(2 * both, pb)],
                far_out.at[c],
                far_in.at[c],
                nxt,
            )

    def send_queries(c):
        send(q_ref.at[:, cols(c)], theirs.at[c, 0], qg_out.at[c], qg_in.at[c], prv)
        send(g_ref.at[:, cols(c)], theirs.at[c, 1], qg_out.at[c], qg_in.at[c], prv)

    def send_sib(c):
        for which, (cont, prompt) in enumerate(((ck_ref, pk_ref), (cv_ref, pv_ref))):
            cont_c, prompt_c = cont.at[:, cols(c)], prompt.at[:, cols(c)]
            send(
                prompt_c, kv.at[c, which, pl.ds(both, pb)], sib_out.at[c], sib_in.at[c], sib
            )
            send(
                cont_c,
                kv.at[c, which, pl.ds(both + pb, cb)],
                sib_out.at[c],
                sib_in.at[c],
                sib,
            )
            pltpu.make_async_copy(cont_c, kv.at[c, which, pl.ds(0, cb)], kv_in.at[c]).start()
            pltpu.make_async_copy(prompt_c, kv.at[c, which, pl.ds(cb, pb)], kv_in.at[c]).start()
        pltpu.make_async_copy(q_ref.at[:, cols(c)], mine.at[c, 0], q_in.at[c]).start()
        pltpu.make_async_copy(g_ref.at[:, cols(c)], mine.at[c, 1], q_in.at[c]).start()

    def rows_of(ref, c, block):
        live = lax.broadcasted_iota(jnp.int32, (cb, 1), 0) < valid_ref[block]
        qs = stacked(ref[c, 0] * jnp.asarray(SCALE, BF16))
        gs = stacked(jnp.where(live, ref[c, 1].astype(F32), 0.0)).astype(BF16)
        return live, qs, gs

    def put_o(c, value):
        out_o[c] = value.astype(BF16)
        pltpu.make_async_copy(out_o.at[c], o_ref.at[:, cols(c)], res_o.at[c]).start()

    def put_dq(c, value):
        out_dq[c] = value.astype(BF16)
        pltpu.make_async_copy(out_dq.at[c], dq_ref.at[:, cols(c)], res_dq.at[c]).start()

    @pl.when(step == 0)
    def _():
        barrier = pltpu.get_barrier_semaphore()

        def greet(other):
            pl.semaphore_signal(barrier, inc=1, device_id={"ctx": other}, device_id_type=MESH)

        greet(sib)

        @pl.when(has_next)
        def _():
            greet(nxt)

        @pl.when(has_prev)
        def _():
            greet(prv)

        @pl.when(has_next & has_prev)
        def _():
            pl.semaphore_wait(barrier, 3)

        @pl.when(jnp.logical_not(has_next & has_prev))
        def _():
            pl.semaphore_wait(barrier, 2)

        @pl.when(jnp.logical_not(has_prev))
        def _():
            got_s[:, 0:1] = jnp.full((chunks, 1, 2 * cb), -1e30, F32)
            got_s[:, 1:2] = jnp.zeros((chunks, 1, 2 * cb), F32)
            got_o[...] = jnp.zeros(got_o.shape, BF16)
            got_dq[...] = jnp.zeros(got_dq.shape, BF16)
            kv[:, :, 2 * both :, :] = jnp.zeros((chunks, 2, pb, PAIR), BF16)

        @pl.when(jnp.logical_not(has_next))
        def _():
            theirs[...] = jnp.zeros(theirs.shape, BF16)
            their_bias[...] = jnp.zeros(their_bias.shape, F32)
            got_back[...] = jnp.zeros(got_back.shape, F32)
            got_far[...] = jnp.zeros(got_far.shape, BF16)


        @pl.when(even & has_prev)
        def _():
            for c in range(QUERY_AHEAD):
                send_queries(c)

        @pl.when(odd & has_next)
        def _():
            for c in range(FAR_AHEAD):
                send_far(c)

        for c in range(SIB_AHEAD):
            send_sib(c)
        near_cont = jnp.where(
            start_ref[0] <= j - 1, valid_ref[jnp.maximum(j - 1, 0)], 0
        )
        own_len = valid_ref[j]
        limits = [jnp.where(links_ref[0, d] > 0, pb, 0) for d in range(3)]
        far_key = lax.broadcasted_iota(jnp.int32, row_bias.shape, 1)
        far_limit = jnp.where(
            far_key < pb,
            limits[2],
            jnp.where(far_key < 2 * pb, limits[1] + pb, near_cont + 2 * pb),
        )
        row_bias[...] = jnp.where(far_key < far_limit, 0.0, -1e30)

        @pl.when(even & has_prev)
        def _():
            send(row_bias, their_bias, rb_out, rb_in, prv)

        key = lax.broadcasted_iota(jnp.int32, (cb, 2 * both + pb), 1)
        query = lax.broadcasted_iota(jnp.int32, (cb, 2 * both + pb), 0)
        limit = jnp.where(
            key < cb,
            jnp.minimum(query, own_len - 1) + 1,
            jnp.where(
                key < both,
                limits[0] + cb,
                jnp.where(
                    key < both + pb,
                    limits[1] + both,
                    jnp.where(
                        key < 2 * both, near_cont + (both + pb), limits[2] + 2 * both
                    ),
                ),
            ),
        )
        bias[...] = jnp.where(key < limit, 0.0, -1e30)

        @pl.when(even & has_next)
        def _():
            wait_bytes(their_bias, rb_in)

    @pl.when((step > 0) & (step + SIB_AHEAD <= chunks))
    def _():
        send_sib(step + SIB_AHEAD - 1)

    @pl.when((step > 0) & (step + QUERY_AHEAD <= chunks) & even & has_prev)
    def _():
        send_queries(step + QUERY_AHEAD - 1)

    @pl.when((step > 0) & (step + FAR_AHEAD <= chunks) & odd & has_next)
    def _():
        send_far(step + FAR_AHEAD - 1)

    @pl.when((step >= RETURN_LAG) & (step < chunks + RETURN_LAG) & odd & has_prev)
    def _():
        c = step - RETURN_LAG
        send(far_g.at[c], got_far.at[c], fg_out.at[c], fg_in.at[c], prv)

    @pl.when((step < chunks) & odd)
    def _():
        c = step
        wait_bytes(own_rows(c), kv_in.at[c])
        wait_bytes(mine.at[c], q_in.at[c])
        wait_bytes(sib_rows(c), sib_in.at[c])

        @pl.when(has_prev)
        def _():
            wait_bytes(far_rows(c), far_in.at[c])

        live, qs, gs = rows_of(mine, c, j)
        k = kv[c, 0]
        v = kv[c, 1]
        b = bias[...]
        s = mm_t(qs, k) + jnp.concatenate([b, b], 0)
        top, total, e, out = softmax_parts(s, v)
        inverse = jnp.broadcast_to(1.0 / total, out.shape)
        out = out * inverse
        put_o(c, jnp.where(live, folded(out), 0.0))
        delta = jnp.broadcast_to(row_dot(gs, out), out.shape)
        dq, grads = gradients(e, qs, gs, k, v, delta, inverse)
        put_dq(c, dq)
        for which in range(2):
            own[lax.rem(c, slots), which] = grads[which][:both]
            sib_g[c, which] = grads[which][both : 2 * both].astype(BF16)
            far_g[c, which] = grads[which][2 * both :].astype(BF16)
        send(sib_g.at[c], got_sib.at[c], sg_out.at[c], sg_in.at[c], sib)

    def wait_first(c):
        wait_bytes(own_rows(c), kv_in.at[c])
        wait_bytes(mine.at[c], q_in.at[c])
        wait_bytes(sib_rows(c), sib_in.at[c])

        @pl.when(has_next)
        def _():
            wait_bytes(theirs.at[c], qg_in.at[c])

    def wait_merge(c):
        @pl.when(has_prev)
        def _():
            wait_bytes(got_s.at[c], s_in.at[c])
            wait_bytes(got_o.at[c], o_in.at[c])

    def wait_back(c):
        @pl.when(has_next)
        def _():
            wait_bytes(got_back.at[c], b_in.at[c])

    def first(c):
        slot = lax.rem(c, e_slots)
        _, qs, gs = rows_of(theirs, c, nxt)
        k = kv[c, 0, cb : 2 * both]
        v = kv[c, 1, cb : 2 * both]
        s = mm_t(qs, k) + their_bias[0:1, :]
        top, total, e, out = softmax_parts(s, v)
        part_o[c] = folded(out * (1.0 / total)).astype(BF16)
        top, total, delta = as_rows(top, total, row_dot(gs, out))
        part_s[c, 0:1] = (top + jnp.log(total)) * LOG2E
        part_s[c, 1:2] = delta / total
        exps[slot] = e
        sums[slot, 0:1] = total

    def merge(c):
        slot = lax.rem(c, slots)
        live, qs, gs = rows_of(mine, c, j)
        k = kv[c, 0, :both]
        v = kv[c, 1, :both]
        b = bias[:, :both]
        s = mm_t(qs, k) + jnp.concatenate([b, b], 0)
        top, total, e, out = softmax_parts(s, v)
        top, total, delta = as_rows(top, total, row_dot(gs, out))
        level = (top + jnp.log(total)) * LOG2E
        far_level = got_s[c, 0:1]
        high = jnp.maximum(level, far_level)
        mix = high + jnp.log(jnp.exp2(level - high) + jnp.exp2(far_level - high)) * LOG2E
        factor = jnp.exp2(level - mix) / total
        far_share = jnp.exp2(far_level - mix)
        delta = factor * delta + far_share * got_s[c, 1:2]
        back_s[c, 0:1] = far_share
        back_s[c, 1:2] = delta
        factor = spread(factor)
        mixed = folded(out * factor) + folded(spread(far_share)) * got_o[c].astype(F32)
        out_o[c] = jnp.where(live, mixed, 0.0).astype(BF16)
        dq, grads = gradients(e, qs, gs, k, v, spread(delta), factor)
        own_dq[slot] = dq
        for which in range(2):
            own[slot, which] = grads[which]

    def back(c):
        slot = lax.rem(c, e_slots)
        _, qs, gs = rows_of(theirs, c, nxt)
        k = kv[c, 0, cb : 2 * both]
        v = kv[c, 1, cb : 2 * both]
        factor = spread(got_back[c, 0:1] / sums[slot, 0:1])
        delta = spread(got_back[c, 1:2])
        dq, grads = gradients(exps[slot], qs, gs, k, v, delta, factor)
        part_dq[c] = dq.astype(BF16)
        for which in range(2):
            own[lax.rem(c, slots), which, cb:, :] += grads[which][:pb]
            sib_g[c, which] = grads[which][pb:].astype(BF16)

    def send_first(c):
        @pl.when(has_next)
        def _():
            send(part_s.at[c], got_s.at[c], s_out.at[c], s_in.at[c], nxt)
            send(part_o.at[c], got_o.at[c], o_out.at[c], o_in.at[c], nxt)

    def send_merge(c):
        @pl.when(has_prev)
        def _():
            send(back_s.at[c], got_back.at[c], b_out.at[c], b_in.at[c], prv)

        pltpu.make_async_copy(out_o.at[c], o_ref.at[:, cols(c)], res_o.at[c]).start()

    def send_back(c):
        @pl.when(has_next)
        def _():
            send(part_dq.at[c], got_dq.at[c], dq_out.at[c], dq_in.at[c], nxt)

        send(sib_g.at[c], got_sib.at[c], sg_out.at[c], sg_in.at[c], sib)

    at_merge = step - MERGE_LAG
    at_back = step - BACK_LAG
    steady = (at_back >= 0) & (step < chunks - 1)

    @pl.when(steady & even)
    def _():
        wait_back(at_back)
        wait_merge(at_merge)
        wait_first(step)
        merge(at_merge)
        back(at_back)
        first(step)
        send_merge(at_merge)
        send_first(step)
        send_back(at_back)

    @pl.when((step < BACK_LAG) & even)
    def _():
        wait_first(step)
        first(step)
        send_first(step)

    @pl.when((at_merge >= 0) & (at_merge < chunks) & even & jnp.logical_not(steady))
    def _():
        wait_merge(at_merge)
        merge(at_merge)
        send_merge(at_merge)

    @pl.when((step >= chunks - 1) & (at_back < chunks) & even)
    def _():
        wait_back(at_back)
        back(at_back)
        send_back(at_back)

    @pl.when((step == chunks - 1) & even)
    def _():
        wait_first(step)
        first(step)
        send_first(step)

    @pl.when(step >= LAG)
    def _():
        c = step - LAG
        slot = lax.rem(c, slots)

        @pl.when(odd)
        def _():
            @pl.when(has_next)
            def _():
                wait_bytes(got_far.at[c], fg_in.at[c])

            own[slot, :, cb:, :] += got_far[c].astype(F32)

        @pl.when(even)
        def _():
            @pl.when(has_prev)
            def _():
                wait_bytes(got_dq.at[c], dq_in.at[c])

            put_dq(c, own_dq[slot] + got_dq[c].astype(F32))

        wait_bytes(got_sib.at[c], sg_in.at[c])
        for which, (cont, prompt) in enumerate(((ckg_ref, pkg_ref), (cvg_ref, pvg_ref))):
            out_g[c, which, :cb, :] = (
                own[slot, which, :cb, :] + got_sib[c, which, pb:, :].astype(F32)
            ).astype(BF16)
            out_g[c, which, cb:, :] = (
                own[slot, which, cb:, :] + got_sib[c, which, :pb, :].astype(F32)
            ).astype(BF16)
            pltpu.make_async_copy(
                out_g.at[c, which, pl.ds(0, cb)], cont.at[:, cols(c)], res_g.at[c]
            ).start()
            pltpu.make_async_copy(
                out_g.at[c, which, pl.ds(cb, pb)], prompt.at[:, cols(c)], res_g.at[c]
            ).start()

    @pl.when(step == chunks + LAG - 1)
    def _():
        def finish(c, carry):
            wait_bytes(sib_rows(c), sib_out.at[c])
            wait_bytes(sib_g.at[c], sg_out.at[c])
            wait_bytes(out_o.at[c], res_o.at[c])
            wait_bytes(out_dq.at[c], res_dq.at[c])
            wait_bytes(out_g.at[c], res_g.at[c])

            @pl.when(even & has_prev)
            def _():
                wait_bytes(theirs.at[c], qg_out.at[c])
                wait_bytes(back_s.at[c], b_out.at[c])

            @pl.when(even & has_next)
            def _():
                wait_bytes(part_o.at[c], o_out.at[c])
                wait_bytes(part_s.at[c], s_out.at[c])
                wait_bytes(part_dq.at[c], dq_out.at[c])

            @pl.when(odd & has_next)
            def _():
                wait_bytes(far_rows(c), far_out.at[c])

            @pl.when(odd & has_prev)
            def _():
                wait_bytes(far_g.at[c], fg_out.at[c])

            return carry

        lax.fori_loop(0, chunks, finish, 0)

        @pl.when(even & has_prev)
        def _():
            wait_bytes(row_bias, rb_out)


def hand_over(*refs):
    count = (len(refs) - 2) // 3
    sources, targets, held = refs[:count], refs[count : 2 * count], refs[2 * count : 3 * count]
    sems_in, sems_out = refs[-2:]
    loads = [
        pltpu.make_async_copy(sources[i], held[i], sems_in.at[i]) for i in range(count)
    ]
    stores = [
        pltpu.make_async_copy(held[i], targets[i], sems_out.at[i]) for i in range(count)
    ]
    for load in loads:
        load.start()
    for load, store in zip(loads, stores):
        load.wait()
        store.start()
    for store in stores:
        store.wait()


def per_device(*args):
    q, ck, cv, pk, pv, g, links, start, valid = args
    cb, width = q.shape
    pb = pk.shape[0]
    chunks = width // PAIR
    length = lax.axis_size("ctx")
    keys = 2 * cb + 3 * pb
    both = cb + pb
    far_keys = cb + 2 * pb
    anywhere = pl.BlockSpec(memory_space=pl.ANY)
    scalars = pl.BlockSpec(memory_space=pltpu.SMEM)
    wide = jax.ShapeDtypeStruct((cb, width), BF16)
    short = jax.ShapeDtypeStruct((pb, width), BF16)
    work = 12 * cb * keys * width
    rows = pltpu.VMEM((chunks, cb, PAIR), BF16)
    stats = pltpu.VMEM((chunks, 2, 2 * cb), F32)
    pair_rows = pltpu.VMEM((chunks, 2, cb, PAIR), BF16)
    sib_grad = pltpu.VMEM((chunks, 2, both, PAIR), BF16)
    far_grad = pltpu.VMEM((chunks, 2, pb, PAIR), BF16)
    results = pl.pallas_call(
        functools.partial(kernel, chunks, length),
        grid=(chunks + LAG,),
        in_specs=[anywhere] * 6 + [scalars] * 3,
        out_specs=[anywhere] * 6,
        out_shape=[wide, wide, wide, wide, short, short],
        scratch_shapes=[
            pltpu.VMEM((chunks, 2, keys, PAIR), BF16),
            pair_rows,
            pair_rows,
            pltpu.VMEM((cb, keys), F32),
            pltpu.VMEM((8, far_keys), F32),
            pltpu.VMEM((8, far_keys), F32),
            pltpu.VMEM((BACK_LAG + 1, 2 * cb, far_keys), BF16),
            pltpu.VMEM((BACK_LAG + 1, 2, 2 * cb), F32),
            pltpu.VMEM((LAG + 1, 2, both, PAIR), F32),
            pltpu.VMEM((LAG + 1, cb, PAIR), F32),
            rows,
            rows,
            stats,
            stats,
            stats,
            stats,
            rows,
            rows,
            sib_grad,
            sib_grad,
            far_grad,
            far_grad,
            rows,
            rows,
            sib_grad,
        ]
        + [pltpu.SemaphoreType.DMA((chunks,))] * 23
        + [pltpu.SemaphoreType.DMA] * 2,
        compiler_params=pltpu.CompilerParams(
            collective_id=0, has_side_effects=True, vmem_limit_bytes=60 * 2**20
        ),
        cost_estimate=pl.CostEstimate(
            flops=work, bytes_accessed=12 * 2 * cb * width, transcendentals=cb * keys * width // HD
        ),
        name="pairs",
    )(q, g, ck, cv, pk, pv, links, start, valid)
    return pl.pallas_call(
        hand_over,
        in_specs=[anywhere] * 6,
        out_specs=[anywhere] * 6,
        out_shape=[wide, wide, wide, wide, short, short],
        scratch_shapes=[pltpu.VMEM(shape.shape, BF16) for shape in (wide,) * 4 + (short,) * 2]
        + [pltpu.SemaphoreType.DMA((6,))] * 2,
        name="hand_over",
    )(*results)


def solution(mesh):
    rows = P(("dp", "ctx"), None)
    return jax.shard_map(
        per_device,
        mesh=mesh,
        in_specs=(rows,) * 7 + (P(("dp", "ctx")), P("dp")),
        out_specs=(rows,) * 6,
        check_vma=False,
    )
```
